32 devices in a mesh: grid: 4 (over y, x), day: 8 (over z, core).
Axes of the slice: x: 2, y: 2, z: 4, core: 2. Of those that a mesh axis runs over, the one named last changes fastest.
Arguments:
- anomalies: bfloat16 [8192, 16384], P('day', 'grid'), may hold values from -6 to 6
- eofs: bfloat16 [64, 16384], P(None, ('grid', 'day')), may hold values from -0.046875 to 0.046875
- means_init: float32 [8, 64], replicated, may hold values from -4 to 4
- variances: float32 [8, 64], replicated, may hold values from 0.05 to 2
- mixing: float32 [8], replicated, may hold values from 0.5 to 2
Outputs:
- regime_means: float32 [8, 64], replicated
- regime_covs: float32 [8, 64, 64], replicated
- regime_weights: float32 [8], replicated
- membership: float32 [8, 8192], P(None, 'day')
- composites: bfloat16 [8, 16384], P(None, ('grid', 'day'))
The draws below stay inside these ranges and needn't reach their ends.
All inputs are finite; a program needn't handle non-finite values.
Results may differ from the reference program's by a relative error of at most 0.0034.
Values may be sent and summed in bfloat16 or wider, within the bound.
A program may use at most 64 MiB of HBM per device.

```python
import math
import jax
import jax.numpy as jnp
from jax import lax

K = 64
R = 8
ITERS = 2
PIX = 16384
DAYS = 8192


def steps_of(key, extent, cuts, smallest, top_value):
    gain = 1.0
    for axis_at, blocks in cuts:
        heights = jax.random.uniform(jax.random.fold_in(jax.random.fold_in(key, 6), axis_at), (blocks,), jnp.float32, smallest / len(cuts), top_value / len(cuts))
        gain = gain * jnp.repeat(jnp.exp(heights), extent[axis_at] // blocks).reshape((-1,) + (1,) * (len(extent) - 1 - axis_at))
    return gain


def bell_draw(rng, dims, deviation, bound, shards=(), held_as=jnp.bfloat16):
    array = jax.random.normal(rng, dims, jnp.float32) * deviation
    if len(shards) > 0:
        array = steps_of(rng, dims, shards, -0.22, 0.18) * array
    return jnp.clip(array, min=-bound, max=bound).astype(held_as)


def setup_inputs(seed: int = 0) -> dict:
    key_of = jax.random.split(jax.random.key(seed), 6)
    return {
        "anomalies": bell_draw(key_of[0], (DAYS, PIX), 1.0, 6.0, ((0, 8), (1, 4))),
        "eofs": bell_draw(key_of[1], (K, PIX), PIX ** -0.5, 0.046875, ((1, 32),)),
        "means_init": bell_draw(key_of[2], (R, K), 1.0, 4.0, (), jnp.float32),
        "variances": jnp.clip(jnp.exp(jax.random.uniform(key_of[3], (R, K), jnp.float32, math.log(0.05), math.log(2.0))), 0.05, 2.0),
        "mixing": jnp.clip(jax.random.uniform(key_of[4], (R,), jnp.float32, 0.5, 2.0), 0.5, 2.0),
    }


PRECISE = lax.Precision.HIGHEST
REG = 0.01

def log_density(pcs_t, means, covs, weights):
    regimes = means.shape[0]
    width = means.shape[1]
    eye = jnp.broadcast_to(jnp.eye(width, dtype=jnp.float32), (regimes, width, width))
    factor = jnp.linalg.cholesky(covs)
    inverse = lax.linalg.triangular_solve(factor, eye, left_side=True, lower=True)
    centred = pcs_t[None, :, :] - means[:, :, None]
    shifted = jnp.einsum('rkj,rjd->rkd', inverse, centred, precision=PRECISE)
    logdet = jnp.sum(jnp.log(jnp.diagonal(factor, axis1=1, axis2=2)), axis=1)
    return jnp.log(weights)[:, None] - logdet[:, None] - 0.5 * jnp.sum(shifted * shifted, axis=1)

def responsibilities(pcs_t, means, covs, weights):
    logp = log_density(pcs_t, means, covs, weights)
    top = jnp.max(logp, axis=0, keepdims=True)
    expo = jnp.exp(logp - top)
    return expo / jnp.sum(expo, axis=0, keepdims=True)

def second_moments(pcs_t, resp, means):
    diff = pcs_t[None, :, :] - means[:, :, None]
    return jnp.einsum('rkd,rjd->rkj', diff * resp[:, None, :], diff, precision=PRECISE)

def reference(anomalies, eofs, means_init, variances, mixing):
    pcs = lax.dot_general(anomalies.astype(jnp.float32), eofs.astype(jnp.float32), (((1,), (1,)), ((), ())), preferred_element_type=jnp.float32)
    pcs_t = pcs.T
    eye = jnp.eye(means_init.shape[1], dtype=jnp.float32)
    means = means_init
    covs = variances[:, :, None] * eye[None]
    weights = mixing / jnp.sum(mixing)
    for step in range(ITERS):
        resp = responsibilities(pcs_t, means, covs, weights)
        counted = jnp.maximum(jnp.sum(resp, axis=1), 1.0)
        means = lax.dot_general(resp, pcs_t, (((1,), (1,)), ((), ())), precision=PRECISE) / counted[:, None]
        covs = second_moments(pcs_t, resp, means) / counted[:, None, None] + REG * eye[None]
        weights = counted / jnp.sum(counted)
    member = responsibilities(pcs_t, means, covs, weights)
    counted = jnp.maximum(jnp.sum(member, axis=1), 1.0)
    sums = jnp.dot(member.astype(jnp.bfloat16).astype(jnp.float32), anomalies.astype(jnp.float32), preferred_element_type=jnp.float32)
    composites = (sums / counted[:, None]).astype(jnp.bfloat16)
    return (means, covs, weights, member, composites)
```

```python
import functools

import jax
import jax.numpy as jnp
from jax import lax
from jax.experimental import pallas as pl
from jax.experimental.pallas import tpu as pltpu
from jax.sharding import PartitionSpec as P

ITERS = 2
REG = 0.01
MESH = pl.DeviceIdType.MESH
PRECISE = lax.Precision.HIGHEST
NT = (((1,), (1,)), ((), ()))


def columns_of(rows):
    width = rows.shape[1]
    i = lax.broadcasted_iota(jnp.int32, (width, width), 0)
    j = lax.broadcasted_iota(jnp.int32, (width, width), 1)
    eye = (i == j).astype(jnp.float32)
    return lax.dot_general(eye, rows, NT, precision=PRECISE, preferred_element_type=jnp.float32)


def softmax_regimes(logp):
    expo = jnp.exp(logp - jnp.max(logp, axis=0, keepdims=True))
    return expo / jnp.sum(expo, axis=0, keepdims=True)


def eliminate(cov):
    width = cov.shape[0]
    blocks = width // 8
    i = lax.broadcasted_iota(jnp.int32, (width, width), 0)
    j = lax.broadcasted_iota(jnp.int32, (width, width), 1)
    eye = (i == j).astype(jnp.float32)
    aug = jnp.concatenate([cov, eye], axis=1)
    rows = [aug[8 * b : 8 * b + 8, :] for b in range(blocks)]
    sub = lax.broadcasted_iota(jnp.int32, (8, 2 * width), 0)
    for step in range(width):
        b, s = step // 8, step % 8
        pivot_row = rows[b][s : s + 1, :]
        scaled = pivot_row * (1.0 / pivot_row[:, step : step + 1])
        for bb in range(b, blocks):
            column = jnp.broadcast_to(rows[bb][:, step : step + 1], (8, 2 * width))
            if bb == b:
                column = jnp.where(sub > s, column, 0.0)
            rows[bb] = rows[bb] - column * scaled
    full = jnp.concatenate(rows, axis=0)
    diag = jnp.sum(full[:, :width] * eye, axis=1, keepdims=True)
    return full * lax.rsqrt(diag), diag


def kernel(
    ng, nd, regimes, width, dl, pb,
    anom_hbm, eofs_ref, means_ref, var_ref, mix_ref,
    o_means, o_covs, o_weights, o_member, o_comp,
    anom, eall, acc, pin, msend, mrecv, gslot, res, cres, memall, csend, crecv,
    anom_sem, e_send, e_fwd, e_recv, p_send, p_recv, m_send, m_recv, g_send, g_recv,
    r_send, r_recv, c_send, c_recv, y_send, y_recv, t_send, t_recv,
):
    g = lax.axis_index("grid")
    d = lax.axis_index("day")
    half = width // 2
    sibling = d + 1 - 2 * lax.rem(d, 2)
    nz = nd // 2

    def day_peer(k):
        return lax.rem(d + k, nd)

    def grid_peer(k):
        return lax.rem(g + k, ng)

    offsets = []
    for k in range(1, nz // 2 + 1):
        offsets.append(k)
        if nz - k != k:
            offsets.append(nz - k)

    def block_pairs():
        pairs = [(d, sibling)]
        for o in offsets:
            same = lax.rem(d + 2 * o, nd)
            pairs.append((same, same + 1 - 2 * lax.rem(same, 2)))
        return pairs

    def load(s):
        return pltpu.make_async_copy(
            anom_hbm.at[:, pl.ds(pl.multiple_of(s * pb, pb), pb)], anom.at[s], anom_sem.at[s]
        )

    pairs = block_pairs()
    for pair in pairs:
        for s in pair:
            load(s).start()

    barrier = pltpu.get_barrier_semaphore()
    for k in range(1, nd):
        pl.semaphore_signal(barrier, inc=1, device_id=(g, day_peer(k)), device_id_type=MESH)
    for k in range(1, ng):
        pl.semaphore_signal(barrier, inc=1, device_id=(grid_peer(k), d), device_id_type=MESH)
    pl.semaphore_wait(barrier, nd - 1 + ng - 1)

    def remote(src, dst, send, recv, target):
        return pltpu.make_async_remote_copy(
            src_ref=src, dst_ref=dst, send_sem=send, recv_sem=recv, device_id=target, device_id_type=MESH
        )

    sent = []

    for n, target in enumerate([lax.rem(d + 2 * o, nd) for o in offsets] + [sibling]):
        copy = remote(eofs_ref, eall.at[d], e_send.at[n], e_recv.at[d], (g, target))
        copy.start()
        sent.append(copy)

    def project(s, block, i):
        days = anom[s, pl.ds(pl.multiple_of(i * dl, dl), dl), :]
        return lax.dot_general(block, days, NT, preferred_element_type=jnp.float32)

    count = 0
    for n, pair in enumerate(pairs):
        for m, s in enumerate(pair):
            if n == 0 and m == 0:
                block = eofs_ref[...]
            else:
                remote(eall.at[s], eall.at[s], e_send.at[0], e_recv.at[s], (g, sibling)).wait_recv()
                if m == 0:
                    copy = remote(eall.at[s], eall.at[s], e_fwd.at[n - 1], e_recv.at[s], (g, sibling))
                    copy.start()
                    sent.append(copy)
                block = eall[s]
            load(s).wait()
            count += 1
            if count < nd:
                first = count == 1

                def add(i, carry):
                    term = project(s, block, i)
                    acc[i] = term if first else acc[i] + term
                    return carry

                if ng <= 4:
                    for i in range(ng):
                        add(i, 0)
                else:
                    lax.fori_loop(0, ng, add, 0)
            else:
                for k in list(range(1, ng)) + [0]:
                    i = grid_peer(k)
                    total = acc[i] + project(s, block, i)
                    if k == 0:
                        pin[g] = total
                    else:
                        acc[i] = total
                        copy = remote(acc.at[i], pin.at[g], p_send.at[k - 1], p_recv.at[g], (i, d))
                        copy.start()
                        sent.append(copy)
    for k in range(1, ng):
        i = grid_peer(k)
        remote(acc.at[i], pin.at[i], p_send.at[k - 1], p_recv.at[i], (i, d)).wait_recv()
    x = pin[0]
    for i in range(1, ng):
        x = x + pin[i]

    means = means_ref[...]
    variances = var_ref[...]
    mix = mix_ref[...]
    mcol = columns_of(means)
    scale = columns_of(lax.rsqrt(variances))
    logw = jnp.log(mix / jnp.sum(mix, axis=0, keepdims=True))
    logdet = 0.5 * jnp.sum(jnp.log(variances), axis=1, keepdims=True)
    quad = []
    for r in range(regimes):
        y = (x - mcol[:, r : r + 1]) * scale[:, r : r + 1]
        quad.append(jnp.sum(y * y, axis=0, keepdims=True))
    resp = softmax_regimes(logw - logdet - 0.5 * jnp.concatenate(quad, axis=0))

    lane = lax.broadcasted_iota(jnp.int32, (8, width), 1)
    ei = lax.broadcasted_iota(jnp.int32, (width, width), 0)
    ej = lax.broadcasted_iota(jnp.int32, (width, width), 1)
    eye = (ei == ej).astype(jnp.float32)

    for it in range(ITERS):
        counts = jnp.sum(resp, axis=1, keepdims=True)
        for r in range(regimes):
            diff = x - mcol[:, r : r + 1]
            lhs = jnp.concatenate([diff * resp[r : r + 1, :], resp], axis=0)
            out = lax.dot_general(lhs, diff, NT, precision=PRECISE, preferred_element_type=jnp.float32)
            msend[it, r, 0:half, :] = jnp.concatenate([out[0:half], out[half:width]], axis=1)
            first = jnp.broadcast_to(out[width + r : width + r + 1, :], (8, width))
            number = jnp.broadcast_to(counts[r : r + 1, :], (8, width))
            msend[it, r, half : half + 8, :] = jnp.concatenate([first, number], axis=1)
            copy = remote(msend.at[it, r], mrecv.at[it, d], m_send.at[it, r], m_recv.at[it, d], (g, r))

            @pl.when(d != r)
            def _():
                copy.start()

        def own():
            mrecv[it, d] = msend[it, d]
            for k in range(1, nd):
                s = day_peer(k)
                remote(mrecv.at[it, s], mrecv.at[it, s], m_send.at[it, 0], m_recv.at[it, s], (g, s)).wait_recv()
            total = mrecv[it, 0]
            for s in range(1, nd):
                total = total + mrecv[it, s]
            gslot[it, g] = total
            for k in range(1, ng):
                copy = remote(gslot.at[it, g], gslot.at[it, g], g_send.at[it, k - 1], g_recv.at[it, g], (grid_peer(k), d))
                copy.start()
            for k in range(1, ng):
                i = grid_peer(k)
                remote(gslot.at[it, i], gslot.at[it, i], g_send.at[it, 0], g_recv.at[it, i], (i, d)).wait_recv()
            total = gslot[it, 0]
            for i in range(1, ng):
                total = total + gslot[it, i]
            second = jnp.concatenate([total[0:half, 0:width], total[0:half, width : 2 * width]], axis=0)
            first = total[half : half + 1, 0:width]
            number = total[half : half + 1, width : 2 * width]
            counted = jnp.maximum(number, 1.0)
            old = means_ref[pl.ds(d, 1), :] if it == 0 else res[it - 1, d, half : half + 1, 0:width]
            delta = (first + (number - counted) * old) / counted
            new = old + delta
            pad = jnp.zeros((6, width), jnp.float32)
            cols = columns_of(jnp.concatenate([delta, first, pad], axis=0))
            dcol, fcol = cols[:, 0:1], cols[:, 1:2]
            moved = second - dcol * first - fcol * delta + dcol * (delta * number)
            cov = moved / counted + REG * eye
            factor, diag = eliminate(cov)
            hld = 0.5 * jnp.sum(jnp.log(diag), axis=0, keepdims=True)
            res[it, d, 0:half, :] = jnp.concatenate(
                [factor[0:half, width : 2 * width], factor[half:width, width : 2 * width]], axis=1
            )
            tail = jnp.where(lane < half, jnp.broadcast_to(counted, (8, width)), jnp.broadcast_to(hld, (8, width)))
            res[it, d, half : half + 8, :] = jnp.concatenate([jnp.broadcast_to(new, (8, width)), tail], axis=1)
            for k in range(1, nd):
                remote(res.at[it, d], res.at[it, d], r_send.at[it, k - 1], r_recv.at[it, d], (g, day_peer(k))).start()
            if it == ITERS - 1:
                cres[d] = jnp.concatenate([cov[0:half], cov[half:width]], axis=1)
                for k in range(1, nd):
                    remote(cres.at[d], cres.at[d], c_send.at[k - 1], c_recv.at[d], (g, day_peer(k))).start()

        if nd > regimes:
            pl.when(d < regimes)(own)
        else:
            own()

        for r in range(regimes):
            @pl.when(d != r)
            def _():
                remote(res.at[it, r], res.at[it, r], r_send.at[it, 0], r_recv.at[it, r], (g, r)).wait_recv()

        means = jnp.concatenate([res[it, r, half : half + 1, 0:width] for r in range(regimes)], axis=0)
        tails = jnp.concatenate([res[it, r, half : half + 1, width : 2 * width] for r in range(regimes)], axis=0)
        counted = tails[:, 0:1]
        weights = counted / jnp.sum(counted, axis=0, keepdims=True)
        mcol = columns_of(means)
        quad = []
        for r in range(regimes):
            folded = res[it, r, 0:half, :]
            factor = jnp.concatenate([folded[:, 0:width], folded[:, width : 2 * width]], axis=0)
            y = jnp.dot(factor, x - mcol[:, r : r + 1], precision=PRECISE, preferred_element_type=jnp.float32)
            quad.append(jnp.sum(y * y, axis=0, keepdims=True))
        logp = jnp.log(weights) - tails[:, half : half + 1] - 0.5 * jnp.concatenate(quad, axis=0)
        resp = softmax_regimes(logp)

    memall[g] = resp
    for k in range(1, ng):
        copy = remote(memall.at[g], memall.at[g], y_send.at[k - 1], y_recv.at[g], (grid_peer(k), d))
        copy.start()
        sent.append(copy)
    o_means[...] = means
    o_weights[...] = weights
    for k in range(1, ng):
        i = grid_peer(k)
        remote(memall.at[i], memall.at[i], y_send.at[0], y_recv.at[i], (i, d)).wait_recv()
    member = jnp.concatenate([memall[i] for i in range(ng)], axis=1)
    o_member[...] = member
    counts = jnp.broadcast_to(jnp.sum(member, axis=1, keepdims=True), (regimes, 128))
    rounded = member.astype(jnp.bfloat16)

    for k in list(range(1, nd)) + [0]:
        s = day_peer(k)
        terms = jnp.dot(rounded, anom[s], preferred_element_type=jnp.float32)
        if k == 0:
            crecv[d, :, 0:pb] = terms
            crecv[d, :, pb : pb + 128] = counts
        else:
            csend[k - 1, :, 0:pb] = terms
            csend[k - 1, :, pb : pb + 128] = counts
            copy = remote(csend.at[k - 1], crecv.at[d], t_send.at[k - 1], t_recv.at[d], (g, s))
            copy.start()
            sent.append(copy)

    for r in range(regimes):
        @pl.when(d != r)
        def _():
            remote(cres.at[r], cres.at[r], c_send.at[0], c_recv.at[r], (g, r)).wait_recv()

        folded = cres[r]
        o_covs[r, 0:half, :] = folded[:, 0:width]
        o_covs[r, half:width, :] = folded[:, width : 2 * width]

    for k in range(1, nd):
        s = day_peer(k)
        remote(crecv.at[s], crecv.at[s], t_send.at[0], t_recv.at[s], (g, s)).wait_recv()
    total = crecv[0]
    for s in range(1, nd):
        total = total + crecv[s]
    o_comp[...] = (total[:, 0:pb] / jnp.maximum(total[:, pb : pb + 1], 1.0)).astype(jnp.bfloat16)

    for copy in sent:
        copy.wait_send()
    for it in range(ITERS):
        for r in range(regimes):
            @pl.when(d != r)
            def _():
                remote(msend.at[it, r], msend.at[it, r], m_send.at[it, r], m_recv.at[it, 0], (g, r)).wait_send()

        def own_sent():
            for k in range(1, ng):
                remote(gslot.at[it, g], gslot.at[it, g], g_send.at[it, k - 1], g_recv.at[it, 0], (grid_peer(k), d)).wait_send()
            for k in range(1, nd):
                remote(res.at[it, d], res.at[it, d], r_send.at[it, k - 1], r_recv.at[it, 0], (g, day_peer(k))).wait_send()
                if it == ITERS - 1:
                    remote(cres.at[d], cres.at[d], c_send.at[k - 1], c_recv.at[0], (g, day_peer(k))).wait_send()

        if nd > regimes:
            pl.when(d < regimes)(own_sent)
        else:
            own_sent()


def solution(mesh):
    ng, nd = mesh.shape["grid"], mesh.shape["day"]

    def body(anomalies, eofs, means_init, variances, mixing):
        days, pixels = anomalies.shape
        width, pb = eofs.shape
        regimes = means_init.shape[0]
        dl = days // ng
        half = width // 2
        f32 = jnp.float32
        vmem = pl.BlockSpec(memory_space=pltpu.VMEM)
        dma = pltpu.SemaphoreType.DMA
        outs = pl.pallas_call(
            functools.partial(kernel, ng, nd, regimes, width, dl, pb),
            out_shape=(
                jax.ShapeDtypeStruct((regimes, width), f32),
                jax.ShapeDtypeStruct((regimes, width, width), f32),
                jax.ShapeDtypeStruct((regimes, 1), f32),
                jax.ShapeDtypeStruct((regimes, days), f32),
                jax.ShapeDtypeStruct((regimes, pb), jnp.bfloat16),
            ),
            in_specs=[pl.BlockSpec(memory_space=pl.ANY)] + [vmem] * 4,
            out_specs=(vmem,) * 5,
            scratch_shapes=[
                pltpu.VMEM((nd, days, pb), jnp.bfloat16),
                pltpu.VMEM((nd, width, pb), jnp.bfloat16),
                pltpu.VMEM((ng, width, dl), f32),
                pltpu.VMEM((ng, width, dl), f32),
                pltpu.VMEM((ITERS, regimes, half + 8, 2 * width), f32),
                pltpu.VMEM((ITERS, nd, half + 8, 2 * width), f32),
                pltpu.VMEM((ITERS, ng, half + 8, 2 * width), f32),
                pltpu.VMEM((ITERS, regimes, half + 8, 2 * width), f32),
                pltpu.VMEM((regimes, half, 2 * width), f32),
                pltpu.VMEM((ng, regimes, dl), f32),
                pltpu.VMEM((nd - 1, regimes, pb + 128), f32),
                pltpu.VMEM((nd, regimes, pb + 128), f32),
                dma((nd,)),
                dma((nd // 2,)),
                dma((nd // 2,)),
                dma((nd,)),
                dma((ng,)),
                dma((ng,)),
                dma((ITERS, regimes)),
                dma((ITERS, nd)),
                dma((ITERS, ng)),
                dma((ITERS, ng)),
                dma((ITERS, nd)),
                dma((ITERS, regimes)),
                dma((nd,)),
                dma((regimes,)),
                dma((ng,)),
                dma((ng,)),
                dma((nd,)),
                dma((nd,)),
            ],
            compiler_params=pltpu.CompilerParams(
                collective_id=0, has_side_effects=True, vmem_limit_bytes=40 * 1024 * 1024
            ),
            name="regimes",
        )(anomalies, eofs, means_init, variances, mixing.reshape(regimes, 1))
        means, covs, weights, member, comp = outs
        return means, covs, weights.reshape(regimes), member, comp

    in_specs = (P("day", "grid"), P(None, ("grid", "day")), P(), P(), P())
    out_specs = (P(), P(), P(), P(None, "day"), P(None, ("grid", "day")))
    return jax.shard_map(body, mesh=mesh, in_specs=in_specs, out_specs=out_specs, check_vma=False)
```

```python
import functools

import jax
import jax.numpy as jnp
from jax import lax
from jax.experimental import pallas as pl
from jax.experimental.pallas import tpu as pltpu
from jax.sharding import PartitionSpec as P

ITERS = 2
REG = 0.01
MESH = pl.DeviceIdType.MESH
PRECISE = lax.Precision.HIGHEST
NT = (((1,), (1,)), ((), ()))


def columns_of(rows):
    width = rows.shape[1]
    i = lax.broadcasted_iota(jnp.int32, (width, width), 0)
    j = lax.broadcasted_iota(jnp.int32, (width, width), 1)
    eye = (i == j).astype(jnp.float32)
    return lax.dot_general(eye, rows, NT, precision=PRECISE, preferred_element_type=jnp.float32)


def softmax_regimes(logp):
    expo = jnp.exp(logp - jnp.max(logp, axis=0, keepdims=True))
    return expo / jnp.sum(expo, axis=0, keepdims=True)


def eliminate(cov):
    width = cov.shape[0]
    blocks = width // 8
    i = lax.broadcasted_iota(jnp.int32, (width, width), 0)
    j = lax.broadcasted_iota(jnp.int32, (width, width), 1)
    eye = (i == j).astype(jnp.float32)
    aug = jnp.concatenate([cov, eye], axis=1)
    rows = [aug[8 * b : 8 * b + 8, :] for b in range(blocks)]
    wide = (8, 2 * width)
    sub = lax.broadcasted_iota(jnp.int32, wide, 0)
    for b in range(blocks):
        cols = [
            [jnp.broadcast_to(rows[bb][:, 8 * b + k : 8 * b + k + 1], wide) for bb in range(b, blocks)]
            for k in range(8)
        ]
        for s in range(8):
            inverse = 1.0 / jnp.broadcast_to(cols[s][0][s : s + 1, :], wide)
            pivot_row = jnp.broadcast_to(rows[b][s : s + 1, :], wide)
            later = [jnp.broadcast_to(cols[k][0][s : s + 1, :], wide) for k in range(s + 1, 8)]
            for n in range(blocks - b):
                column = cols[s][n]
                if n == 0:
                    column = jnp.where(sub > s, column, 0.0)
                factor = column * inverse
                for k in range(s + 1, 8):
                    cols[k][n] = cols[k][n] - factor * later[k - s - 1]
                rows[b + n] = rows[b + n] - factor * pivot_row
    full = jnp.concatenate(rows, axis=0)
    diag = jnp.sum(full[:, :width] * eye, axis=1, keepdims=True)
    return full * lax.rsqrt(diag), diag


def kernel(
    ng, nd, regimes, width, dl, pb,
    anom_hbm, eofs_ref, means_hbm, var_hbm, mix_hbm,
    o_means, o_covs, o_weights, o_member, o_comp,
    means_ref, var_ref, mix_ref, anom, eall, acc, pin, msend, mrecv, gslot, res, cres, memall, csend, crecv,
    anom_sem, e_send, e_fwd, e_recv, p_send, p_recv, m_send, m_recv, g_send, g_recv,
    r_send, r_recv, c_send, c_recv, y_send, y_recv, t_send, t_recv, i_sem,
):
    g = lax.axis_index("grid")
    d = lax.axis_index("day")
    half = width // 2
    sibling = d + 1 - 2 * lax.rem(d, 2)
    nz = nd // 2

    def day_peer(k):
        return lax.rem(d + k, nd)

    def grid_peer(k):
        return lax.rem(g + k, ng)

    offsets = []
    for k in range(1, nz // 2 + 1):
        offsets.append(k)
        if nz - k != k:
            offsets.append(nz - k)

    def block_pairs():
        pairs = [(d, sibling)]
        for o in offsets:
            same = lax.rem(d + 2 * o, nd)
            pairs.append((same, same + 1 - 2 * lax.rem(same, 2)))
        return pairs

    def load(s):
        return pltpu.make_async_copy(
            anom_hbm.at[:, pl.ds(pl.multiple_of(s * pb, pb), pb)], anom.at[s], anom_sem.at[s]
        )

    first_copies = [
        pltpu.make_async_copy(eofs_ref, eall.at[d], i_sem.at[0]),
        pltpu.make_async_copy(means_hbm, means_ref, i_sem.at[1]),
        pltpu.make_async_copy(var_hbm, var_ref, i_sem.at[2]),
        pltpu.make_async_copy(mix_hbm, mix_ref, i_sem.at[3]),
    ]
    for copy in first_copies:
        copy.start()
    pairs = block_pairs()
    for pair in pairs:
        for s in pair:
            load(s).start()

    barrier = pltpu.get_barrier_semaphore()
    for k in range(1, nd):
        pl.semaphore_signal(barrier, inc=1, device_id=(g, day_peer(k)), device_id_type=MESH)
    for k in range(1, ng):
        pl.semaphore_signal(barrier, inc=1, device_id=(grid_peer(k), d), device_id_type=MESH)
    pl.semaphore_wait(barrier, nd - 1 + ng - 1)

    def remote(src, dst, send, recv, target):
        return pltpu.make_async_remote_copy(
            src_ref=src, dst_ref=dst, send_sem=send, recv_sem=recv, device_id=target, device_id_type=MESH
        )

    sent = []

    for n, target in enumerate([lax.rem(d + 2 * o, nd) for o in offsets] + [sibling]):
        copy = remote(eofs_ref, eall.at[d], e_send.at[n], e_recv.at[d], (g, target))
        copy.start()
        sent.append(copy)

    def project(s, block, i):
        days = anom[s, pl.ds(pl.multiple_of(i * dl, dl), dl), :]
        return lax.dot_general(block, days, NT, preferred_element_type=jnp.float32)

    count = 0
    for n, pair in enumerate(pairs):
        for m, s in enumerate(pair):
            if n == 0 and m == 0:
                first_copies[0].wait()
                block = eall[s]
            else:
                remote(eall.at[s], eall.at[s], e_send.at[0], e_recv.at[s], (g, sibling)).wait_recv()
                if m == 0:
                    copy = remote(eall.at[s], eall.at[s], e_fwd.at[n - 1], e_recv.at[s], (g, sibling))
                    copy.start()
                    sent.append(copy)
                block = eall[s]
            load(s).wait()
            count += 1
            if count < nd:
                first = count == 1

                def add(i, carry):
                    term = project(s, block, i)
                    acc[i] = term if first else acc[i] + term
                    return carry

                if ng <= 4:
                    for i in range(ng):
                        add(i, 0)
                else:
                    lax.fori_loop(0, ng, add, 0)
            else:
                for k in list(range(1, ng)) + [0]:
                    i = grid_peer(k)
                    total = acc[i] + project(s, block, i)
                    if k == 0:
                        pin[g] = total
                    else:
                        acc[i] = total
                        copy = remote(acc.at[i], pin.at[g], p_send.at[k - 1], p_recv.at[g], (i, d))
                        copy.start()
                        sent.append(copy)
    for k in range(1, ng):
        i = grid_peer(k)
        remote(acc.at[i], pin.at[i], p_send.at[k - 1], p_recv.at[i], (i, d)).wait_recv()
    x = pin[0]
    for i in range(1, ng):
        x = x + pin[i]

    for copy in first_copies[1:]:
        copy.wait()
    means = means_ref[...]
    variances = var_ref[...]
    er = lax.broadcasted_iota(jnp.int32, (regimes, regimes), 0)
    ec = lax.broadcasted_iota(jnp.int32, (regimes, regimes), 1)
    mix = jnp.sum(jnp.where(er == ec, mix_ref[...].reshape(1, regimes), 0.0), axis=1, keepdims=True)
    mcol = columns_of(means)
    scale = columns_of(lax.rsqrt(variances))
    logw = jnp.log(mix / jnp.sum(mix, axis=0, keepdims=True))
    logdet = 0.5 * jnp.sum(jnp.log(variances), axis=1, keepdims=True)
    quad = []
    for r in range(regimes):
        y = (x - mcol[:, r : r + 1]) * scale[:, r : r + 1]
        quad.append(jnp.sum(y * y, axis=0, keepdims=True))
    resp = softmax_regimes(logw - logdet - 0.5 * jnp.concatenate(quad, axis=0))

    lane = lax.broadcasted_iota(jnp.int32, (8, width), 1)
    ei = lax.broadcasted_iota(jnp.int32, (width, width), 0)
    ej = lax.broadcasted_iota(jnp.int32, (width, width), 1)
    eye = (ei == ej).astype(jnp.float32)

    for it in range(ITERS):
        counts = jnp.sum(resp, axis=1, keepdims=True)
        for r in range(regimes):
            diff = x - mcol[:, r : r + 1]
            lhs = jnp.concatenate([diff * resp[r : r + 1, :], resp], axis=0)
            out = lax.dot_general(lhs, diff, NT, precision=PRECISE, preferred_element_type=jnp.float32)
            msend[it, r, 0:half, :] = jnp.concatenate([out[0:half], out[half:width]], axis=1)
            first = jnp.broadcast_to(out[width + r : width + r + 1, :], (8, width))
            number = jnp.broadcast_to(counts[r : r + 1, :], (8, width))
            msend[it, r, half : half + 8, :] = jnp.concatenate([first, number], axis=1)
            copy = remote(msend.at[it, r], mrecv.at[it, d], m_send.at[it, r], m_recv.at[it, d], (g, r))

            @pl.when(d != r)
            def _():
                copy.start()

        def own():
            mrecv[it, d] = msend[it, d]
            for k in range(1, nd):
                s = day_peer(k)
                remote(mrecv.at[it, s], mrecv.at[it, s], m_send.at[it, 0], m_recv.at[it, s], (g, s)).wait_recv()
            total = mrecv[it, 0]
            for s in range(1, nd):
                total = total + mrecv[it, s]
            gslot[it, g] = total
            for k in range(1, ng):
                copy = remote(gslot.at[it, g], gslot.at[it, g], g_send.at[it, k - 1], g_recv.at[it, g], (grid_peer(k), d))
                copy.start()
            for k in range(1, ng):
                i = grid_peer(k)
                remote(gslot.at[it, i], gslot.at[it, i], g_send.at[it, 0], g_recv.at[it, i], (i, d)).wait_recv()
            total = gslot[it, 0]
            for i in range(1, ng):
                total = total + gslot[it, i]
            second = jnp.concatenate([total[0:half, 0:width], total[0:half, width : 2 * width]], axis=0)
            first = total[half : half + 1, 0:width]
            number = total[half : half + 1, width : 2 * width]
            counted = jnp.maximum(number, 1.0)
            old = means_ref[pl.ds(d, 1), :] if it == 0 else res[it - 1, d, half : half + 1, 0:width]
            delta = (first + (number - counted) * old) / counted
            new = old + delta
            pad = jnp.zeros((6, width), jnp.float32)
            cols = columns_of(jnp.concatenate([delta, first, pad], axis=0))
            dcol, fcol = cols[:, 0:1], cols[:, 1:2]
            moved = second - dcol * first - fcol * delta + dcol * (delta * number)
            cov = moved / counted + REG * eye
            factor, diag = eliminate(cov)
            hld = 0.5 * jnp.sum(jnp.log(diag), axis=0, keepdims=True)
            res[it, d, 0:half, :] = jnp.concatenate(
                [factor[0:half, width : 2 * width], factor[half:width, width : 2 * width]], axis=1
            )
            tail = jnp.where(lane < half, jnp.broadcast_to(counted, (8, width)), jnp.broadcast_to(hld, (8, width)))
            res[it, d, half : half + 8, :] = jnp.concatenate([jnp.broadcast_to(new, (8, width)), tail], axis=1)
            for k in range(1, nd):
                remote(res.at[it, d], res.at[it, d], r_send.at[it, k - 1], r_recv.at[it, d], (g, day_peer(k))).start()
            if it == ITERS - 1:
                cres[d] = jnp.concatenate([cov[0:half], cov[half:width]], axis=1)
                for k in range(1, nd):
                    remote(cres.at[d], cres.at[d], c_send.at[k - 1], c_recv.at[d], (g, day_peer(k))).start()

        if nd > regimes:
            pl.when(d < regimes)(own)
        else:
            own()

        for r in range(regimes):
            @pl.when(d != r)
            def _():
                remote(res.at[it, r], res.at[it, r], r_send.at[it, 0], r_recv.at[it, r], (g, r)).wait_recv()

        means = jnp.concatenate([res[it, r, half : half + 1, 0:width] for r in range(regimes)], axis=0)
        tails = jnp.concatenate([res[it, r, half : half + 1, width : 2 * width] for r in range(regimes)], axis=0)
        counted = tails[:, 0:1]
        weights = counted / jnp.sum(counted, axis=0, keepdims=True)
        mcol = columns_of(means)
        quad = []
        for r in range(regimes):
            folded = res[it, r, 0:half, :]
            factor = jnp.concatenate([folded[:, 0:width], folded[:, width : 2 * width]], axis=0)
            y = jnp.dot(factor, x - mcol[:, r : r + 1], precision=PRECISE, preferred_element_type=jnp.float32)
            quad.append(jnp.sum(y * y, axis=0, keepdims=True))
        logp = jnp.log(weights) - tails[:, half : half + 1] - 0.5 * jnp.concatenate(quad, axis=0)
        resp = softmax_regimes(logp)

    memall[g] = resp
    for k in range(1, ng):
        copy = remote(memall.at[g], memall.at[g], y_send.at[k - 1], y_recv.at[g], (grid_peer(k), d))
        copy.start()
        sent.append(copy)
    o_means[...] = means
    o_weights[...] = jnp.sum(jnp.where(er == ec, weights, 0.0), axis=0)
    for k in range(1, ng):
        i = grid_peer(k)
        remote(memall.at[i], memall.at[i], y_send.at[0], y_recv.at[i], (i, d)).wait_recv()
    member = jnp.concatenate([memall[i] for i in range(ng)], axis=1)
    o_member[...] = member
    counts = jnp.broadcast_to(jnp.sum(member, axis=1, keepdims=True), (regimes, 128))
    rounded = member.astype(jnp.bfloat16)

    for k in list(range(1, nd)) + [0]:
        s = day_peer(k)
        terms = jnp.dot(rounded, anom[s], preferred_element_type=jnp.float32)
        if k == 0:
            crecv[d, :, 0:pb] = terms
            crecv[d, :, pb : pb + 128] = counts
        else:
            csend[k - 1, :, 0:pb] = terms
            csend[k - 1, :, pb : pb + 128] = counts
            copy = remote(csend.at[k - 1], crecv.at[d], t_send.at[k - 1], t_recv.at[d], (g, s))
            copy.start()
            sent.append(copy)

    for r in range(regimes):
        @pl.when(d != r)
        def _():
            remote(cres.at[r], cres.at[r], c_send.at[0], c_recv.at[r], (g, r)).wait_recv()

        folded = cres[r]
        o_covs[r, 0:half, :] = folded[:, 0:width]
        o_covs[r, half:width, :] = folded[:, width : 2 * width]

    for k in range(1, nd):
        s = day_peer(k)
        remote(crecv.at[s], crecv.at[s], t_send.at[0], t_recv.at[s], (g, s)).wait_recv()
    total = crecv[0]
    for s in range(1, nd):
        total = total + crecv[s]
    o_comp[...] = (total[:, 0:pb] / jnp.maximum(total[:, pb : pb + 1], 1.0)).astype(jnp.bfloat16)

    for copy in sent:
        copy.wait_send()
    for it in range(ITERS):
        for r in range(regimes):
            @pl.when(d != r)
            def _():
                remote(msend.at[it, r], msend.at[it, r], m_send.at[it, r], m_recv.at[it, 0], (g, r)).wait_send()

        def own_sent():
            for k in range(1, ng):
                remote(gslot.at[it, g], gslot.at[it, g], g_send.at[it, k - 1], g_recv.at[it, 0], (grid_peer(k), d)).wait_send()
            for k in range(1, nd):
                remote(res.at[it, d], res.at[it, d], r_send.at[it, k - 1], r_recv.at[it, 0], (g, day_peer(k))).wait_send()
                if it == ITERS - 1:
                    remote(cres.at[d], cres.at[d], c_send.at[k - 1], c_recv.at[0], (g, day_peer(k))).wait_send()

        if nd > regimes:
            pl.when(d < regimes)(own_sent)
        else:
            own_sent()


def solution(mesh):
    ng, nd = mesh.shape["grid"], mesh.shape["day"]

    def body(anomalies, eofs, means_init, variances, mixing):
        days, pixels = anomalies.shape
        width, pb = eofs.shape
        regimes = means_init.shape[0]
        dl = days // ng
        half = width // 2
        f32 = jnp.float32
        vmem = pl.BlockSpec(memory_space=pltpu.VMEM)
        dma = pltpu.SemaphoreType.DMA
        outs = pl.pallas_call(
            functools.partial(kernel, ng, nd, regimes, width, dl, pb),
            out_shape=(
                jax.ShapeDtypeStruct((regimes, width), f32),
                jax.ShapeDtypeStruct((regimes, width, width), f32),
                jax.ShapeDtypeStruct((regimes,), f32),
                jax.ShapeDtypeStruct((regimes, days), f32),
                jax.ShapeDtypeStruct((regimes, pb), jnp.bfloat16),
            ),
            in_specs=[pl.BlockSpec(memory_space=pltpu.HBM)] * 5,
            out_specs=(vmem,) * 5,
            scratch_shapes=[
                pltpu.VMEM((regimes, width), f32),
                pltpu.VMEM((regimes, width), f32),
                pltpu.VMEM((regimes,), f32),
                pltpu.VMEM((nd, days, pb), jnp.bfloat16),
                pltpu.VMEM((nd, width, pb), jnp.bfloat16),
                pltpu.VMEM((ng, width, dl), f32),
                pltpu.VMEM((ng, width, dl), f32),
                pltpu.VMEM((ITERS, regimes, half + 8, 2 * width), f32),
                pltpu.VMEM((ITERS, nd, half + 8, 2 * width), f32),
                pltpu.VMEM((ITERS, ng, half + 8, 2 * width), f32),
                pltpu.VMEM((ITERS, regimes, half + 8, 2 * width), f32),
                pltpu.VMEM((regimes, half, 2 * width), f32),
                pltpu.VMEM((ng, regimes, dl), f32),
                pltpu.VMEM((nd - 1, regimes, pb + 128), f32),
                pltpu.VMEM((nd, regimes, pb + 128), f32),
                dma((nd,)),
                dma((nd // 2,)),
                dma((nd // 2,)),
                dma((nd,)),
                dma((ng,)),
                dma((ng,)),
                dma((ITERS, regimes)),
                dma((ITERS, nd)),
                dma((ITERS, ng)),
                dma((ITERS, ng)),
                dma((ITERS, nd)),
                dma((ITERS, regimes)),
                dma((nd,)),
                dma((regimes,)),
                dma((ng,)),
                dma((ng,)),
                dma((nd,)),
                dma((nd,)),
                dma((4,)),
            ],
            compiler_params=pltpu.CompilerParams(
                collective_id=0, has_side_effects=True, vmem_limit_bytes=48 * 1024 * 1024
            ),
            name="regimes",
        )(anomalies, eofs, means_init, variances, mixing)
        return outs

    in_specs = (P("day", "grid"), P(None, ("grid", "day")), P(), P(), P())
    out_specs = (P(), P(), P(), P(None, "day"), P(None, ("grid", "day")))
    return jax.shard_map(body, mesh=mesh, in_specs=in_specs, out_specs=out_specs, check_vma=False)
```

```python
import functools

import jax
import jax.numpy as jnp
from jax import lax
from jax.experimental import pallas as pl
from jax.experimental.pallas import tpu as pltpu
from jax.sharding import PartitionSpec as P

ITERS = 2
REG = 0.01
MESH = pl.DeviceIdType.MESH
PRECISE = lax.Precision.HIGHEST
NT = (((1,), (1,)), ((), ()))


def columns_of(rows):
    width = rows.shape[1]
    i = lax.broadcasted_iota(jnp.int32, (width, width), 0)
    j = lax.broadcasted_iota(jnp.int32, (width, width), 1)
    eye = (i == j).astype(jnp.float32)
    return lax.dot_general(eye, rows, NT, precision=PRECISE, preferred_element_type=jnp.float32)


def softmax_regimes(logp):
    expo = jnp.exp(logp - jnp.max(logp, axis=0, keepdims=True))
    return expo / jnp.sum(expo, axis=0, keepdims=True)


def eliminate(cov):
    width = cov.shape[0]
    blocks = width // 8
    i = lax.broadcasted_iota(jnp.int32, (width, width), 0)
    j = lax.broadcasted_iota(jnp.int32, (width, width), 1)
    eye = (i == j).astype(jnp.float32)
    aug = jnp.concatenate([cov, eye], axis=1)
    rows = [aug[8 * b : 8 * b + 8, :] for b in range(blocks)]
    wide = (8, 2 * width)
    sub = lax.broadcasted_iota(jnp.int32, wide, 0)
    for b in range(blocks):
        cols = [
            [jnp.broadcast_to(rows[bb][:, 8 * b + k : 8 * b + k + 1], wide) for bb in range(b, blocks)]
            for k in range(8)
        ]
        for s in range(8):
            inverse = 1.0 / jnp.broadcast_to(cols[s][0][s : s + 1, :], wide)
            pivot_row = jnp.broadcast_to(rows[b][s : s + 1, :], wide)
            later = [jnp.broadcast_to(cols[k][0][s : s + 1, :], wide) for k in range(s + 1, 8)]
            for n in range(blocks - b):
                column = cols[s][n]
                if n == 0:
                    column = jnp.where(sub > s, column, 0.0)
                factor = column * inverse
                for k in range(s + 1, 8):
                    cols[k][n] = cols[k][n] - factor * later[k - s - 1]
                rows[b + n] = rows[b + n] - factor * pivot_row
    full = jnp.concatenate(rows, axis=0)
    diag = jnp.sum(full[:, :width] * eye, axis=1, keepdims=True)
    return full * lax.rsqrt(diag), diag


def kernel(
    ng, nd, regimes, width, dl, pb,
    anom_hbm, eofs_ref, means_hbm, var_hbm, mix_hbm,
    o_means, o_covs, o_weights, o_member, o_comp,
    means_ref, var_ref, mix_ref, anom, eall, acc, pin, msend, msib, chip, mrecv, gslot, res, cres, memall, cout, cin, csend, crecv, cnt,
    anom_sem, e_send, e_fwd, e_recv, p_send, p_recv, s_send, s_recv, m_send, m_recv, g_send, g_recv,
    r_send, r_fwd, r_recv, c_send, c_fwd, c_recv, y_send, y_recv, u_send, u_recv, t_send, t_recv, n_send, n_recv, i_sem,
):
    g = lax.axis_index("grid")
    d = lax.axis_index("day")
    half = width // 2
    sibling = d + 1 - 2 * lax.rem(d, 2)
    nz = nd // 2
    pairs_of = regimes // 2
    core = lax.rem(d, 2)
    z = lax.div(d, 2)

    def day_peer(k):
        return lax.rem(d + k, nd)

    def grid_peer(k):
        return lax.rem(g + k, ng)

    offsets = []
    for k in range(1, nz // 2 + 1):
        offsets.append(k)
        if nz - k != k:
            offsets.append(nz - k)

    def block_pairs():
        pairs = [(d, sibling)]
        for o in offsets:
            same = lax.rem(d + 2 * o, nd)
            pairs.append((same, same + 1 - 2 * lax.rem(same, 2)))
        return pairs

    def load(s):
        return pltpu.make_async_copy(
            anom_hbm.at[:, pl.ds(pl.multiple_of(s * pb, pb), pb)], anom.at[s], anom_sem.at[s]
        )

    first_copies = [
        pltpu.make_async_copy(eofs_ref, eall.at[d], i_sem.at[0]),
        pltpu.make_async_copy(means_hbm, means_ref, i_sem.at[1]),
        pltpu.make_async_copy(var_hbm, var_ref, i_sem.at[2]),
        pltpu.make_async_copy(mix_hbm, mix_ref, i_sem.at[3]),
    ]
    for copy in first_copies:
        copy.start()
    pairs = block_pairs()
    for pair in pairs:
        for s in pair:
            load(s).start()

    barrier = pltpu.get_barrier_semaphore()
    for k in range(1, nd):
        pl.semaphore_signal(barrier, inc=1, device_id=(g, day_peer(k)), device_id_type=MESH)
    for k in range(1, ng):
        pl.semaphore_signal(barrier, inc=1, device_id=(grid_peer(k), d), device_id_type=MESH)
    pl.semaphore_wait(barrier, nd - 1 + ng - 1)

    def remote(src, dst, send, recv, target):
        return pltpu.make_async_remote_copy(
            src_ref=src, dst_ref=dst, send_sem=send, recv_sem=recv, device_id=target, device_id_type=MESH
        )

    sent = []

    near = [lax.rem(d + 2 * o, nd) for o in offsets] + [sibling]
    for n, target in enumerate(near):
        copy = remote(eofs_ref, eall.at[d], e_send.at[n], e_recv.at[d], (g, target))
        copy.start()
        sent.append(copy)

    def project(s, block, i):
        days = anom[s, pl.ds(pl.multiple_of(i * dl, dl), dl), :]
        return lax.dot_general(block, days, NT, preferred_element_type=jnp.float32)

    count = 0
    for n, pair in enumerate(pairs):
        for m, s in enumerate(pair):
            if n == 0 and m == 0:
                first_copies[0].wait()
                block = eall[s]
            else:
                remote(eall.at[s], eall.at[s], e_send.at[0], e_recv.at[s], (g, sibling)).wait_recv()
                if m == 0:
                    copy = remote(eall.at[s], eall.at[s], e_fwd.at[n - 1], e_recv.at[s], (g, sibling))
                    copy.start()
                    sent.append(copy)
                block = eall[s]
            load(s).wait()
            count += 1
            if count < nd:
                first = count == 1

                def add(i, carry):
                    term = project(s, block, i)
                    acc[i] = term if first else acc[i] + term
                    return carry

                if ng <= 4:
                    for i in range(ng):
                        add(i, 0)
                else:
                    lax.fori_loop(0, ng, add, 0)
            else:
                for k in list(range(1, ng)) + [0]:
                    i = grid_peer(k)
                    total = acc[i] + project(s, block, i)
                    if k == 0:
                        pin[g] = total
                    else:
                        acc[i] = total
                        copy = remote(acc.at[i], pin.at[g], p_send.at[k - 1], p_recv.at[g], (i, d))
                        copy.start()
                        sent.append(copy)
    for k in range(1, ng):
        i = grid_peer(k)
        remote(acc.at[i], pin.at[i], p_send.at[k - 1], p_recv.at[i], (i, d)).wait_recv()
    x = pin[0]
    for i in range(1, ng):
        x = x + pin[i]

    for copy in first_copies[1:]:
        copy.wait()
    means = means_ref[...]
    variances = var_ref[...]
    er = lax.broadcasted_iota(jnp.int32, (regimes, regimes), 0)
    ec = lax.broadcasted_iota(jnp.int32, (regimes, regimes), 1)
    mix = jnp.sum(jnp.where(er == ec, mix_ref[...].reshape(1, regimes), 0.0), axis=1, keepdims=True)
    mcol = columns_of(means)
    scale = columns_of(lax.rsqrt(variances))
    logw = jnp.log(mix / jnp.sum(mix, axis=0, keepdims=True))
    logdet = 0.5 * jnp.sum(jnp.log(variances), axis=1, keepdims=True)
    quad = []
    for r in range(regimes):
        y = (x - mcol[:, r : r + 1]) * scale[:, r : r + 1]
        quad.append(jnp.sum(y * y, axis=0, keepdims=True))
    resp = softmax_regimes(logw - logdet - 0.5 * jnp.concatenate(quad, axis=0))

    lane = lax.broadcasted_iota(jnp.int32, (8, width), 1)
    ei = lax.broadcasted_iota(jnp.int32, (width, width), 0)
    ej = lax.broadcasted_iota(jnp.int32, (width, width), 1)
    eye = (ei == ej).astype(jnp.float32)

    for it in range(ITERS):
        counts = jnp.sum(resp, axis=1, keepdims=True)
        for r in range(regimes):
            diff = x - mcol[:, r : r + 1]
            lhs = jnp.concatenate([diff * resp[r : r + 1, :], resp], axis=0)
            out = lax.dot_general(lhs, diff, NT, precision=PRECISE, preferred_element_type=jnp.float32)
            msend[it, r, 0:half, :] = jnp.concatenate([out[0:half], out[half:width]], axis=1)
            first = jnp.broadcast_to(out[width + r : width + r + 1, :], (8, width))
            number = jnp.broadcast_to(counts[r : r + 1, :], (8, width))
            msend[it, r, half : half + 8, :] = jnp.concatenate([first, number], axis=1)

            @pl.when(core != r % 2)
            def _():
                remote(msend.at[it, r], msib.at[it, r // 2], s_send.at[it, r // 2], s_recv.at[it, r // 2], (g, sibling)).start()

        for n in range(pairs_of):
            mine = 2 * n + core
            remote(msib.at[it, n], msib.at[it, n], s_send.at[it, n], s_recv.at[it, n], (g, sibling)).wait_recv()
            chip[it, n] = msend[it, mine] + msib[it, n]

            @pl.when(z != n)
            def _():
                remote(chip.at[it, n], mrecv.at[it, z], m_send.at[it, n], m_recv.at[it, z], (g, mine)).start()

        def own():
            mrecv[it, z] = chip[it, z]
            for k in range(1, nz):
                s = lax.rem(z + k, nz)
                remote(mrecv.at[it, s], mrecv.at[it, s], m_send.at[it, 0], m_recv.at[it, s], (g, sibling)).wait_recv()
            total = mrecv[it, 0]
            for s in range(1, nz):
                total = total + mrecv[it, s]
            gslot[it, g] = total
            for k in range(1, ng):
                copy = remote(gslot.at[it, g], gslot.at[it, g], g_send.at[it, k - 1], g_recv.at[it, g], (grid_peer(k), d))
                copy.start()
            for k in range(1, ng):
                i = grid_peer(k)
                remote(gslot.at[it, i], gslot.at[it, i], g_send.at[it, 0], g_recv.at[it, i], (i, d)).wait_recv()
            total = gslot[it, 0]
            for i in range(1, ng):
                total = total + gslot[it, i]
            second = jnp.concatenate([total[0:half, 0:width], total[0:half, width : 2 * width]], axis=0)
            first = total[half : half + 1, 0:width]
            number = total[half : half + 1, width : 2 * width]
            counted = jnp.maximum(number, 1.0)
            old = means_ref[pl.ds(d, 1), :] if it == 0 else res[it - 1, d, half : half + 1, 0:width]
            delta = (first + (number - counted) * old) / counted
            new = old + delta
            pad = jnp.zeros((6, width), jnp.float32)
            cols = columns_of(jnp.concatenate([delta, first, pad], axis=0))
            dcol, fcol = cols[:, 0:1], cols[:, 1:2]
            moved = second - dcol * first - fcol * delta + dcol * (delta * number)
            cov = moved / counted + REG * eye
            factor, diag = eliminate(cov)
            hld = 0.5 * jnp.sum(jnp.log(diag), axis=0, keepdims=True)
            res[it, d, 0:half, :] = jnp.concatenate(
                [factor[0:half, width : 2 * width], factor[half:width, width : 2 * width]], axis=1
            )
            tail = jnp.where(lane < half, jnp.broadcast_to(counted, (8, width)), jnp.broadcast_to(hld, (8, width)))
            res[it, d, half : half + 8, :] = jnp.concatenate([jnp.broadcast_to(new, (8, width)), tail], axis=1)
            for n, target in enumerate(near):
                remote(res.at[it, d], res.at[it, d], r_send.at[it, n], r_recv.at[it, d], (g, target)).start()
            if it == ITERS - 1:
                cres[d] = jnp.concatenate([cov[0:half], cov[half:width]], axis=1)
                for n, target in enumerate(near):
                    remote(cres.at[d], cres.at[d], c_send.at[n], c_recv.at[d], (g, target)).start()

        if nd > regimes:
            pl.when(d < regimes)(own)
        else:
            own()

        for n in range(pairs_of):
            r = 2 * n + core

            @pl.when(z != n)
            def _():
                copy = remote(res.at[it, r], res.at[it, r], r_fwd.at[it, n], r_recv.at[it, r], (g, sibling))
                copy.wait_recv()
                copy.start()

        for n in range(pairs_of):
            r = 2 * n + 1 - core
            remote(res.at[it, r], res.at[it, r], r_fwd.at[it, n], r_recv.at[it, r], (g, sibling)).wait_recv()

        means = jnp.concatenate([res[it, r, half : half + 1, 0:width] for r in range(regimes)], axis=0)
        tails = jnp.concatenate([res[it, r, half : half + 1, width : 2 * width] for r in range(regimes)], axis=0)
        counted = tails[:, 0:1]
        weights = counted / jnp.sum(counted, axis=0, keepdims=True)
        mcol = columns_of(means)
        quad = []
        for r in range(regimes):
            folded = res[it, r, 0:half, :]
            factor = jnp.concatenate([folded[:, 0:width], folded[:, width : 2 * width]], axis=0)
            y = jnp.dot(factor, x - mcol[:, r : r + 1], precision=PRECISE, preferred_element_type=jnp.float32)
            quad.append(jnp.sum(y * y, axis=0, keepdims=True))
        logp = jnp.log(weights) - tails[:, half : half + 1] - 0.5 * jnp.concatenate(quad, axis=0)
        resp = softmax_regimes(logp)

    memall[g] = resp
    for k in range(1, ng):
        copy = remote(memall.at[g], memall.at[g], y_send.at[k - 1], y_recv.at[g], (grid_peer(k), d))
        copy.start()
        sent.append(copy)
    o_means[...] = means
    o_weights[...] = jnp.sum(jnp.where(er == ec, weights, 0.0), axis=0)
    for k in range(1, ng):
        i = grid_peer(k)
        remote(memall.at[i], memall.at[i], y_send.at[0], y_recv.at[i], (i, d)).wait_recv()
    member = jnp.concatenate([memall[i] for i in range(ng)], axis=1)
    o_member[...] = member
    cnt[d] = jnp.broadcast_to(jnp.sum(member, axis=1, keepdims=True), (regimes, 128))
    for k in range(1, nd):
        copy = remote(cnt.at[d], cnt.at[d], n_send.at[k - 1], n_recv.at[d], (g, day_peer(k)))
        copy.start()
        sent.append(copy)
    rounded = member.astype(jnp.bfloat16)

    order = [lax.rem(z + o, nz) for o in reversed(offsets)] + [z]
    for n in order:
        cout[n] = jnp.dot(rounded, anom[2 * n + 1 - core], preferred_element_type=jnp.float32)
        copy = remote(cout.at[n], cin.at[n], u_send.at[n], u_recv.at[n], (g, sibling))
        copy.start()
        sent.append(copy)

    for n in range(pairs_of):
        r = 2 * n + core

        @pl.when(z != n)
        def _():
            copy = remote(cres.at[r], cres.at[r], c_fwd.at[n], c_recv.at[r], (g, sibling))
            copy.wait_recv()
            copy.start()

    for n in order:
        terms = jnp.dot(rounded, anom[2 * n + core], preferred_element_type=jnp.float32)
        remote(cin.at[n], cin.at[n], u_send.at[n], u_recv.at[n], (g, sibling)).wait_recv()
        terms = terms + cin[n]
        if n is z:
            crecv[z] = terms
        else:
            csend[n] = terms
            copy = remote(csend.at[n], crecv.at[z], t_send.at[n], t_recv.at[z], (g, 2 * n + core))
            copy.start()
            sent.append(copy)

    for n in range(pairs_of):
        r = 2 * n + 1 - core
        remote(cres.at[r], cres.at[r], c_fwd.at[n], c_recv.at[r], (g, sibling)).wait_recv()
    for r in range(regimes):
        folded = cres[r]
        o_covs[r, 0:half, :] = folded[:, 0:width]
        o_covs[r, half:width, :] = folded[:, width : 2 * width]

    for k in range(1, nd):
        s = day_peer(k)
        remote(cnt.at[s], cnt.at[s], n_send.at[0], n_recv.at[s], (g, s)).wait_recv()
    number = cnt[0]
    for s in range(1, nd):
        number = number + cnt[s]
    for n in order[:-1]:
        remote(crecv.at[n], crecv.at[n], t_send.at[n], t_recv.at[n], (g, sibling)).wait_recv()
    total = crecv[0]
    for n in range(1, nz):
        total = total + crecv[n]
    o_comp[...] = (total / jnp.maximum(number[:, 0:1], 1.0)).astype(jnp.bfloat16)

    for copy in sent:
        copy.wait_send()
    for it in range(ITERS):
        for n in range(pairs_of):
            r = 2 * n + core
            remote(msend.at[it, r], msib.at[it, n], s_send.at[it, n], s_recv.at[it, n], (g, sibling)).wait_send()

            @pl.when(z != n)
            def _():
                remote(chip.at[it, n], mrecv.at[it, z], m_send.at[it, n], m_recv.at[it, z], (g, r)).wait_send()
                remote(res.at[it, r], res.at[it, r], r_fwd.at[it, n], r_recv.at[it, r], (g, sibling)).wait_send()
                if it == ITERS - 1:
                    remote(cres.at[r], cres.at[r], c_fwd.at[n], c_recv.at[r], (g, sibling)).wait_send()

        def own_sent():
            for k in range(1, ng):
                remote(gslot.at[it, g], gslot.at[it, g], g_send.at[it, k - 1], g_recv.at[it, 0], (grid_peer(k), d)).wait_send()
            for n, target in enumerate(near):
                remote(res.at[it, d], res.at[it, d], r_send.at[it, n], r_recv.at[it, d], (g, target)).wait_send()
                if it == ITERS - 1:
                    remote(cres.at[d], cres.at[d], c_send.at[n], c_recv.at[d], (g, target)).wait_send()

        if nd > regimes:
            pl.when(d < regimes)(own_sent)
        else:
            own_sent()


def hand_over(*refs):
    n = (len(refs) - 1) // 2
    copies = [pltpu.make_async_copy(refs[i], refs[n + i], refs[-1].at[i]) for i in range(n)]
    for copy in copies:
        copy.start()
    for copy in copies:
        copy.wait()


def solution(mesh):
    ng, nd = mesh.shape["grid"], mesh.shape["day"]

    def body(anomalies, eofs, means_init, variances, mixing):
        days, pixels = anomalies.shape
        width, pb = eofs.shape
        regimes = means_init.shape[0]
        dl = days // ng
        half = width // 2
        nz = nd // 2
        f32 = jnp.float32
        vmem = pl.BlockSpec(memory_space=pltpu.VMEM)
        dma = pltpu.SemaphoreType.DMA
        outs = pl.pallas_call(
            functools.partial(kernel, ng, nd, regimes, width, dl, pb),
            out_shape=(
                jax.ShapeDtypeStruct((regimes, width), f32),
                jax.ShapeDtypeStruct((regimes, width, width), f32),
                jax.ShapeDtypeStruct((regimes,), f32),
                jax.ShapeDtypeStruct((regimes, days), f32),
                jax.ShapeDtypeStruct((regimes, pb), jnp.bfloat16),
            ),
            in_specs=[pl.BlockSpec(memory_space=pltpu.HBM)] * 5,
            out_specs=(vmem,) * 5,
            scratch_shapes=[
                pltpu.VMEM((regimes, width), f32),
                pltpu.VMEM((regimes, width), f32),
                pltpu.VMEM((regimes,), f32),
                pltpu.VMEM((nd, days, pb), jnp.bfloat16),
                pltpu.VMEM((nd, width, pb), jnp.bfloat16),
                pltpu.VMEM((ng, width, dl), f32),
                pltpu.VMEM((ng, width, dl), f32),
                pltpu.VMEM((ITERS, regimes, half + 8, 2 * width), f32),
                pltpu.VMEM((ITERS, regimes // 2, half + 8, 2 * width), f32),
                pltpu.VMEM((ITERS, regimes // 2, half + 8, 2 * width), f32),
                pltpu.VMEM((ITERS, nz, half + 8, 2 * width), f32),
                pltpu.VMEM((ITERS, ng, half + 8, 2 * width), f32),
                pltpu.VMEM((ITERS, regimes, half + 8, 2 * width), f32),
                pltpu.VMEM((regimes, half, 2 * width), f32),
                pltpu.VMEM((ng, regimes, dl), f32),
                pltpu.VMEM((nz, regimes, pb), f32),
                pltpu.VMEM((nz, regimes, pb), f32),
                pltpu.VMEM((nz, regimes, pb), f32),
                pltpu.VMEM((nz, regimes, pb), f32),
                pltpu.VMEM((nd, regimes, 128), f32),
                dma((nd,)),
                dma((nz,)),
                dma((nz,)),
                dma((nd,)),
                dma((ng,)),
                dma((ng,)),
                dma((ITERS, regimes // 2)),
                dma((ITERS, regimes // 2)),
                dma((ITERS, regimes // 2)),
                dma((ITERS, nz)),
                dma((ITERS, ng)),
                dma((ITERS, ng)),
                dma((ITERS, nz)),
                dma((ITERS, regimes // 2)),
                dma((ITERS, regimes)),
                dma((nz,)),
                dma((regimes // 2,)),
                dma((regimes,)),
                dma((ng,)),
                dma((ng,)),
                dma((nz,)),
                dma((nz,)),
                dma((nz,)),
                dma((nz,)),
                dma((nd,)),
                dma((nd,)),
                dma((4,)),
            ],
            compiler_params=pltpu.CompilerParams(
                collective_id=0, has_side_effects=True, vmem_limit_bytes=60 * 1024 * 1024
            ),
            name="regimes",
        )(anomalies, eofs, means_init, variances, mixing)
        anywhere = pl.BlockSpec(memory_space=pltpu.HBM)
        return pl.pallas_call(
            hand_over,
            out_shape=tuple(jax.ShapeDtypeStruct(o.shape, o.dtype) for o in outs),
            in_specs=[anywhere] * len(outs),
            out_specs=(anywhere,) * len(outs),
            scratch_shapes=[dma((len(outs),))],
            compiler_params=pltpu.CompilerParams(vmem_limit_bytes=60 * 1024 * 1024),
            name="hand_over",
        )(*outs)

    in_specs = (P("day", "grid"), P(None, ("grid", "day")), P(), P(), P())
    out_specs = (P(), P(), P(), P(None, "day"), P(None, ("grid", "day")))
    return jax.shard_map(body, mesh=mesh, in_specs=in_specs, out_specs=out_specs, check_vma=False)
```

```python
import functools

import jax
import jax.numpy as jnp
from jax import lax
from jax.experimental import pallas as pl
from jax.experimental.pallas import tpu as pltpu
from jax.sharding import PartitionSpec as P

ITERS = 2
REG = 0.01
MESH = pl.DeviceIdType.MESH
PRECISE = lax.Precision.HIGHEST
NT = (((1,), (1,)), ((), ()))


def columns_of(rows):
    width = rows.shape[1]
    i = lax.broadcasted_iota(jnp.int32, (width, width), 0)
    j = lax.broadcasted_iota(jnp.int32, (width, width), 1)
    eye = (i == j).astype(jnp.float32)
    return lax.dot_general(eye, rows, NT, precision=PRECISE, preferred_element_type=jnp.float32)


def softmax_regimes(logp):
    expo = jnp.exp(logp - jnp.max(logp, axis=0, keepdims=True))
    return expo / jnp.sum(expo, axis=0, keepdims=True)


def eliminate(cov):
    width = cov.shape[0]
    blocks = width // 8
    i = lax.broadcasted_iota(jnp.int32, (width, width), 0)
    j = lax.broadcasted_iota(jnp.int32, (width, width), 1)
    eye = (i == j).astype(jnp.float32)
    aug = jnp.concatenate([cov, eye], axis=1)
    rows = [aug[8 * b : 8 * b + 8, :] for b in range(blocks)]
    wide = (8, 2 * width)
    sub = lax.broadcasted_iota(jnp.int32, wide, 0)
    for b in range(blocks):
        cols = [
            [jnp.broadcast_to(rows[bb][:, 8 * b + k : 8 * b + k + 1], wide) for bb in range(b, blocks)]
            for k in range(8)
        ]
        for s in range(8):
            inverse = 1.0 / jnp.broadcast_to(cols[s][0][s : s + 1, :], wide)
            pivot_row = jnp.broadcast_to(rows[b][s : s + 1, :], wide)
            later = [jnp.broadcast_to(cols[k][0][s : s + 1, :], wide) for k in range(s + 1, 8)]
            for n in range(blocks - b):
                column = cols[s][n]
                if n == 0:
                    column = jnp.where(sub > s, column, 0.0)
                factor = column * inverse
                for k in range(s + 1, 8):
                    cols[k][n] = cols[k][n] - factor * later[k - s - 1]
                rows[b + n] = rows[b + n] - factor * pivot_row
    full = jnp.concatenate(rows, axis=0)
    diag = jnp.sum(full[:, :width] * eye, axis=1, keepdims=True)
    return full * lax.rsqrt(diag), diag


def kernel(
    ng, nd, regimes, width, dl, pb,
    anom_hbm, eofs_ref, means_hbm, var_hbm, mix_hbm,
    o_means, o_covs, o_weights, o_member, o_comp,
    means_ref, var_ref, mix_ref, anom, eall, acc, pout, pin, msend, msib, chip, mrecv, gslot, res, cres, memall, cacc, cout, cin, csend, crecv, cnt,
    anom_sem, e_send, e_fwd, e_recv, p_send, p_recv, s_send, s_recv, m_send, m_recv, g_send, g_recv,
    r_send, r_fwd, r_recv, c_send, c_fwd, c_recv, y_send, y_recv, u_send, u_recv, t_send, t_recv, n_send, n_recv, i_sem,
):
    g = lax.axis_index("grid")
    d = lax.axis_index("day")
    half = width // 2
    sibling = d + 1 - 2 * lax.rem(d, 2)
    nz = nd // 2
    pairs_of = regimes // 2
    core = lax.rem(d, 2)
    z = lax.div(d, 2)

    def day_peer(k):
        return lax.rem(d + k, nd)

    def grid_peer(k):
        return lax.rem(g + k, ng)

    offsets = []
    for k in range(1, nz // 2 + 1):
        offsets.append(k)
        if nz - k != k:
            offsets.append(nz - k)

    def block_pairs():
        pairs = [(d, sibling)]
        for o in offsets:
            same = lax.rem(d + 2 * o, nd)
            pairs.append((same, same + 1 - 2 * lax.rem(same, 2)))
        return pairs

    def load(s):
        return pltpu.make_async_copy(
            anom_hbm.at[:, pl.ds(pl.multiple_of(s * pb, pb), pb)], anom.at[s], anom_sem.at[s]
        )

    first_copies = [
        pltpu.make_async_copy(eofs_ref, eall.at[d], i_sem.at[0]),
        pltpu.make_async_copy(means_hbm, means_ref, i_sem.at[1]),
        pltpu.make_async_copy(var_hbm, var_ref, i_sem.at[2]),
        pltpu.make_async_copy(mix_hbm, mix_ref, i_sem.at[3]),
    ]
    for copy in first_copies:
        copy.start()
    pairs = block_pairs()
    for pair in pairs:
        for s in pair:
            load(s).start()

    barrier = pltpu.get_barrier_semaphore()
    for k in range(1, nd):
        pl.semaphore_signal(barrier, inc=1, device_id=(g, day_peer(k)), device_id_type=MESH)
    for k in range(1, ng):
        pl.semaphore_signal(barrier, inc=1, device_id=(grid_peer(k), d), device_id_type=MESH)
    pl.semaphore_wait(barrier, nd - 1 + ng - 1)

    def remote(src, dst, send, recv, target):
        return pltpu.make_async_remote_copy(
            src_ref=src, dst_ref=dst, send_sem=send, recv_sem=recv, device_id=target, device_id_type=MESH
        )

    sent = []

    near = [lax.rem(d + 2 * o, nd) for o in offsets] + [sibling]
    for n, target in enumerate(near):
        copy = remote(eofs_ref, eall.at[d], e_send.at[n], e_recv.at[d], (g, target))
        copy.start()
        sent.append(copy)

    def part(i):
        return pl.ds(pl.multiple_of(i * dl, dl), dl)

    count = 0
    for n, pair in enumerate(pairs):
        for m, s in enumerate(pair):
            if n == 0 and m == 0:
                first_copies[0].wait()
                block = eall[s]
            else:
                remote(eall.at[s], eall.at[s], e_send.at[0], e_recv.at[s], (g, sibling)).wait_recv()
                if m == 0:
                    copy = remote(eall.at[s], eall.at[s], e_fwd.at[n - 1], e_recv.at[s], (g, sibling))
                    copy.start()
                    sent.append(copy)
                block = eall[s]
            load(s).wait()
            count += 1
            if count < nd:
                term = lax.dot_general(anom[s], block, NT, preferred_element_type=jnp.float32)
                acc[...] = term if count == 1 else acc[...] + term
            else:
                for k in list(range(1, ng)) + [0]:
                    i = grid_peer(k)
                    term = lax.dot_general(anom[s, part(i), :], block, NT, preferred_element_type=jnp.float32)
                    total = (acc[part(i), :] + term).T
                    if k == 0:
                        pin[g] = total
                    else:
                        pout[i] = total
                        copy = remote(pout.at[i], pin.at[g], p_send.at[k - 1], p_recv.at[g], (i, d))
                        copy.start()
                        sent.append(copy)
    for k in range(1, ng):
        i = grid_peer(k)
        remote(pout.at[i], pin.at[i], p_send.at[k - 1], p_recv.at[i], (i, d)).wait_recv()
    x = pin[0]
    for i in range(1, ng):
        x = x + pin[i]

    for copy in first_copies[1:]:
        copy.wait()
    means = means_ref[...]
    variances = var_ref[...]
    er = lax.broadcasted_iota(jnp.int32, (regimes, regimes), 0)
    ec = lax.broadcasted_iota(jnp.int32, (regimes, regimes), 1)
    mix = jnp.sum(jnp.where(er == ec, mix_ref[...].reshape(1, regimes), 0.0), axis=1, keepdims=True)
    mcol = columns_of(means)
    scale = columns_of(lax.rsqrt(variances))
    logw = jnp.log(mix / jnp.sum(mix, axis=0, keepdims=True))
    logdet = 0.5 * jnp.sum(jnp.log(variances), axis=1, keepdims=True)
    quad = []
    for r in range(regimes):
        y = (x - mcol[:, r : r + 1]) * scale[:, r : r + 1]
        quad.append(jnp.sum(y * y, axis=0, keepdims=True))
    resp = softmax_regimes(logw - logdet - 0.5 * jnp.concatenate(quad, axis=0))

    lane = lax.broadcasted_iota(jnp.int32, (8, width), 1)
    ei = lax.broadcasted_iota(jnp.int32, (width, width), 0)
    ej = lax.broadcasted_iota(jnp.int32, (width, width), 1)
    eye = (ei == ej).astype(jnp.float32)

    for it in range(ITERS):
        counts = jnp.sum(resp, axis=1, keepdims=True)
        for r in range(regimes):
            diff = x - mcol[:, r : r + 1]
            lhs = jnp.concatenate([diff * resp[r : r + 1, :], resp], axis=0)
            out = lax.dot_general(lhs, diff, NT, precision=PRECISE, preferred_element_type=jnp.float32)
            msend[it, r, 0:half, :] = jnp.concatenate([out[0:half], out[half:width]], axis=1)
            first = jnp.broadcast_to(out[width + r : width + r + 1, :], (8, width))
            number = jnp.broadcast_to(counts[r : r + 1, :], (8, width))
            msend[it, r, half : half + 8, :] = jnp.concatenate([first, number], axis=1)

            @pl.when(core != r % 2)
            def _():
                remote(msend.at[it, r], msib.at[it, r // 2], s_send.at[it, r // 2], s_recv.at[it, r // 2], (g, sibling)).start()

        for n in range(pairs_of):
            mine = 2 * n + core
            remote(msib.at[it, n], msib.at[it, n], s_send.at[it, n], s_recv.at[it, n], (g, sibling)).wait_recv()
            chip[it, n] = msend[it, mine] + msib[it, n]

            @pl.when(z != n)
            def _():
                remote(chip.at[it, n], mrecv.at[it, z], m_send.at[it, n], m_recv.at[it, z], (g, mine)).start()

        def own():
            mrecv[it, z] = chip[it, z]
            for k in range(1, nz):
                s = lax.rem(z + k, nz)
                remote(mrecv.at[it, s], mrecv.at[it, s], m_send.at[it, 0], m_recv.at[it, s], (g, sibling)).wait_recv()
            total = mrecv[it, 0]
            for s in range(1, nz):
                total = total + mrecv[it, s]
            gslot[it, g] = total
            for k in range(1, ng):
                copy = remote(gslot.at[it, g], gslot.at[it, g], g_send.at[it, k - 1], g_recv.at[it, g], (grid_peer(k), d))
                copy.start()
            for k in range(1, ng):
                i = grid_peer(k)
                remote(gslot.at[it, i], gslot.at[it, i], g_send.at[it, 0], g_recv.at[it, i], (i, d)).wait_recv()
            total = gslot[it, 0]
            for i in range(1, ng):
                total = total + gslot[it, i]
            second = jnp.concatenate([total[0:half, 0:width], total[0:half, width : 2 * width]], axis=0)
            first = total[half : half + 1, 0:width]
            number = total[half : half + 1, width : 2 * width]
            counted = jnp.maximum(number, 1.0)
            old = means_ref[pl.ds(d, 1), :] if it == 0 else res[it - 1, d, half : half + 1, 0:width]
            delta = (first + (number - counted) * old) / counted
            new = old + delta
            pad = jnp.zeros((6, width), jnp.float32)
            cols = columns_of(jnp.concatenate([delta, first, pad], axis=0))
            dcol, fcol = cols[:, 0:1], cols[:, 1:2]
            moved = second - dcol * first - fcol * delta + dcol * (delta * number)
            cov = moved / counted + REG * eye
            factor, diag = eliminate(cov)
            hld = 0.5 * jnp.sum(jnp.log(diag), axis=0, keepdims=True)
            res[it, d, 0:half, :] = jnp.concatenate(
                [factor[0:half, width : 2 * width], factor[half:width, width : 2 * width]], axis=1
            )
            tail = jnp.where(lane < half, jnp.broadcast_to(counted, (8, width)), jnp.broadcast_to(hld, (8, width)))
            res[it, d, half : half + 8, :] = jnp.concatenate([jnp.broadcast_to(new, (8, width)), tail], axis=1)
            for n, target in enumerate(near):
                remote(res.at[it, d], res.at[it, d], r_send.at[it, n], r_recv.at[it, d], (g, target)).start()
            if it == ITERS - 1:
                cres[d] = jnp.concatenate([cov[0:half], cov[half:width]], axis=1)
                for n, target in enumerate(near):
                    remote(cres.at[d], cres.at[d], c_send.at[n], c_recv.at[d], (g, target)).start()

        if nd > regimes:
            pl.when(d < regimes)(own)
        else:
            own()

        for n in range(pairs_of):
            r = 2 * n + core

            @pl.when(z != n)
            def _():
                copy = remote(res.at[it, r], res.at[it, r], r_fwd.at[it, n], r_recv.at[it, r], (g, sibling))
                copy.wait_recv()
                copy.start()

        for n in range(pairs_of):
            r = 2 * n + 1 - core
            remote(res.at[it, r], res.at[it, r], r_fwd.at[it, n], r_recv.at[it, r], (g, sibling)).wait_recv()

        means = jnp.concatenate([res[it, r, half : half + 1, 0:width] for r in range(regimes)], axis=0)
        tails = jnp.concatenate([res[it, r, half : half + 1, width : 2 * width] for r in range(regimes)], axis=0)
        counted = tails[:, 0:1]
        weights = counted / jnp.sum(counted, axis=0, keepdims=True)
        mcol = columns_of(means)
        quad = []
        for r in range(regimes):
            folded = res[it, r, 0:half, :]
            factor = jnp.concatenate([folded[:, 0:width], folded[:, width : 2 * width]], axis=0)
            y = jnp.dot(factor, x - mcol[:, r : r + 1], precision=PRECISE, preferred_element_type=jnp.float32)
            quad.append(jnp.sum(y * y, axis=0, keepdims=True))
        logp = jnp.log(weights) - tails[:, half : half + 1] - 0.5 * jnp.concatenate(quad, axis=0)
        resp = softmax_regimes(logp)

    memall[g] = resp
    for k in range(1, ng):
        copy = remote(memall.at[g], memall.at[g], y_send.at[k - 1], y_recv.at[g], (grid_peer(k), d))
        copy.start()
        sent.append(copy)
    mine = resp.astype(jnp.bfloat16)
    for s in range(nd):
        cacc[s] = jnp.dot(mine, anom[s, part(g), :], preferred_element_type=jnp.float32)
    o_means[...] = means
    o_weights[...] = jnp.sum(jnp.where(er == ec, weights, 0.0), axis=0)
    for k in range(1, ng):
        i = grid_peer(k)
        remote(memall.at[i], memall.at[i], y_send.at[0], y_recv.at[i], (i, d)).wait_recv()
    member = jnp.concatenate([memall[i] for i in range(ng)], axis=1)
    o_member[...] = member
    cnt[d] = jnp.broadcast_to(jnp.sum(member, axis=1, keepdims=True), (regimes, 128))
    for k in range(1, nd):
        copy = remote(cnt.at[d], cnt.at[d], n_send.at[k - 1], n_recv.at[d], (g, day_peer(k)))
        copy.start()
        sent.append(copy)

    def field_sums(s):
        def add(k, total):
            i = grid_peer(k)
            days = memall[i].astype(jnp.bfloat16)
            return total + jnp.dot(days, anom[s, part(i), :], preferred_element_type=jnp.float32)

        total = cacc[s]
        if ng > 4:
            return lax.fori_loop(1, ng, add, total)
        for k in range(1, ng):
            total = add(k, total)
        return total

    order = [lax.rem(z + o, nz) for o in reversed(offsets)] + [z]
    for n in order:
        cout[n] = field_sums(2 * n + 1 - core)
        copy = remote(cout.at[n], cin.at[n], u_send.at[n], u_recv.at[n], (g, sibling))
        copy.start()
        sent.append(copy)

    for n in range(pairs_of):
        r = 2 * n + core

        @pl.when(z != n)
        def _():
            copy = remote(cres.at[r], cres.at[r], c_fwd.at[n], c_recv.at[r], (g, sibling))
            copy.wait_recv()
            copy.start()

    for n in order:
        terms = field_sums(2 * n + core)
        remote(cin.at[n], cin.at[n], u_send.at[n], u_recv.at[n], (g, sibling)).wait_recv()
        terms = terms + cin[n]
        if n is z:
            crecv[z] = terms
        else:
            csend[n] = terms
            copy = remote(csend.at[n], crecv.at[z], t_send.at[n], t_recv.at[z], (g, 2 * n + core))
            copy.start()
            sent.append(copy)

    for n in range(pairs_of):
        r = 2 * n + 1 - core
        remote(cres.at[r], cres.at[r], c_fwd.at[n], c_recv.at[r], (g, sibling)).wait_recv()
    for r in range(regimes):
        folded = cres[r]
        o_covs[r, 0:half, :] = folded[:, 0:width]
        o_covs[r, half:width, :] = folded[:, width : 2 * width]

    for k in range(1, nd):
        s = day_peer(k)
        remote(cnt.at[s], cnt.at[s], n_send.at[0], n_recv.at[s], (g, s)).wait_recv()
    number = cnt[0]
    for s in range(1, nd):
        number = number + cnt[s]
    for n in order[:-1]:
        remote(crecv.at[n], crecv.at[n], t_send.at[n], t_recv.at[n], (g, sibling)).wait_recv()
    total = crecv[0]
    for n in range(1, nz):
        total = total + crecv[n]
    o_comp[...] = (total / jnp.maximum(number[:, 0:1], 1.0)).astype(jnp.bfloat16)

    for copy in sent:
        copy.wait_send()
    for it in range(ITERS):
        for n in range(pairs_of):
            r = 2 * n + core
            remote(msend.at[it, r], msib.at[it, n], s_send.at[it, n], s_recv.at[it, n], (g, sibling)).wait_send()

            @pl.when(z != n)
            def _():
                remote(chip.at[it, n], mrecv.at[it, z], m_send.at[it, n], m_recv.at[it, z], (g, r)).wait_send()
                remote(res.at[it, r], res.at[it, r], r_fwd.at[it, n], r_recv.at[it, r], (g, sibling)).wait_send()
                if it == ITERS - 1:
                    remote(cres.at[r], cres.at[r], c_fwd.at[n], c_recv.at[r], (g, sibling)).wait_send()

        def own_sent():
            for k in range(1, ng):
                remote(gslot.at[it, g], gslot.at[it, g], g_send.at[it, k - 1], g_recv.at[it, 0], (grid_peer(k), d)).wait_send()
            for n, target in enumerate(near):
                remote(res.at[it, d], res.at[it, d], r_send.at[it, n], r_recv.at[it, d], (g, target)).wait_send()
                if it == ITERS - 1:
                    remote(cres.at[d], cres.at[d], c_send.at[n], c_recv.at[d], (g, target)).wait_send()

        if nd > regimes:
            pl.when(d < regimes)(own_sent)
        else:
            own_sent()


def hand_over(*refs):
    n = len(refs) // 2
    for i in range(n):
        refs[n + i][...] = refs[i][...]


def solution(mesh):
    ng, nd = mesh.shape["grid"], mesh.shape["day"]

    def body(anomalies, eofs, means_init, variances, mixing):
        days, pixels = anomalies.shape
        width, pb = eofs.shape
        regimes = means_init.shape[0]
        dl = days // ng
        half = width // 2
        nz = nd // 2
        f32 = jnp.float32
        vmem = pl.BlockSpec(memory_space=pltpu.VMEM)
        dma = pltpu.SemaphoreType.DMA
        outs = pl.pallas_call(
            functools.partial(kernel, ng, nd, regimes, width, dl, pb),
            out_shape=(
                jax.ShapeDtypeStruct((regimes, width), f32),
                jax.ShapeDtypeStruct((regimes, width, width), f32),
                jax.ShapeDtypeStruct((regimes,), f32),
                jax.ShapeDtypeStruct((regimes, days), f32),
                jax.ShapeDtypeStruct((regimes, pb), jnp.bfloat16),
            ),
            in_specs=[pl.BlockSpec(memory_space=pltpu.HBM)] * 5,
            out_specs=(vmem,) * 5,
            scratch_shapes=[
                pltpu.VMEM((regimes, width), f32),
                pltpu.VMEM((regimes, width), f32),
                pltpu.VMEM((regimes,), f32),
                pltpu.VMEM((nd, days, pb), jnp.bfloat16),
                pltpu.VMEM((nd, width, pb), jnp.bfloat16),
                pltpu.VMEM((days, width), f32),
                pltpu.VMEM((ng, width, dl), f32),
                pltpu.VMEM((ng, width, dl), f32),
                pltpu.VMEM((ITERS, regimes, half + 8, 2 * width), f32),
                pltpu.VMEM((ITERS, regimes // 2, half + 8, 2 * width), f32),
                pltpu.VMEM((ITERS, regimes // 2, half + 8, 2 * width), f32),
                pltpu.VMEM((ITERS, nz, half + 8, 2 * width), f32),
                pltpu.VMEM((ITERS, ng, half + 8, 2 * width), f32),
                pltpu.VMEM((ITERS, regimes, half + 8, 2 * width), f32),
                pltpu.VMEM((regimes, half, 2 * width), f32),
                pltpu.VMEM((ng, regimes, dl), f32),
                pltpu.VMEM((nd, regimes, pb), f32),
                pltpu.VMEM((nz, regimes, pb), f32),
                pltpu.VMEM((nz, regimes, pb), f32),
                pltpu.VMEM((nz, regimes, pb), f32),
                pltpu.VMEM((nz, regimes, pb), f32),
                pltpu.VMEM((nd, regimes, 128), f32),
                dma((nd,)),
                dma((nz,)),
                dma((nz,)),
                dma((nd,)),
                dma((ng,)),
                dma((ng,)),
                dma((ITERS, regimes // 2)),
                dma((ITERS, regimes // 2)),
                dma((ITERS, regimes // 2)),
                dma((ITERS, nz)),
                dma((ITERS, ng)),
                dma((ITERS, ng)),
                dma((ITERS, nz)),
                dma((ITERS, regimes // 2)),
                dma((ITERS, regimes)),
                dma((nz,)),
                dma((regimes // 2,)),
                dma((regimes,)),
                dma((ng,)),
                dma((ng,)),
                dma((nz,)),
                dma((nz,)),
                dma((nz,)),
                dma((nz,)),
                dma((nd,)),
                dma((nd,)),
                dma((4,)),
            ],
            compiler_params=pltpu.CompilerParams(
                collective_id=0, has_side_effects=True, vmem_limit_bytes=60 * 1024 * 1024
            ),
            name="regimes",
        )(anomalies, eofs, means_init, variances, mixing)
        return pl.pallas_call(
            hand_over,
            out_shape=tuple(jax.ShapeDtypeStruct(o.shape, o.dtype) for o in outs),
            in_specs=[vmem] * len(outs),
            out_specs=(vmem,) * len(outs),
            compiler_params=pltpu.CompilerParams(vmem_limit_bytes=60 * 1024 * 1024),
            name="hand_over",
        )(*outs)

    in_specs = (P("day", "grid"), P(None, ("grid", "day")), P(), P(), P())
    out_specs = (P(), P(), P(), P(None, "day"), P(None, ("grid", "day")))
    return jax.shard_map(body, mesh=mesh, in_specs=in_specs, out_specs=out_specs, check_vma=False)
```

```python
import functools

import jax
import jax.numpy as jnp
from jax import lax
from jax.experimental import pallas as pl
from jax.experimental.pallas import tpu as pltpu
from jax.sharding import PartitionSpec as P

ITERS = 2
REG = 0.01
MESH = pl.DeviceIdType.MESH
PRECISE = lax.Precision.HIGHEST
NT = (((1,), (1,)), ((), ()))


def columns_of(rows):
    width = rows.shape[1]
    i = lax.broadcasted_iota(jnp.int32, (width, width), 0)
    j = lax.broadcasted_iota(jnp.int32, (width, width), 1)
    eye = (i == j).astype(jnp.float32)
    return lax.dot_general(eye, rows, NT, precision=PRECISE, preferred_element_type=jnp.float32)


def softmax_regimes(logp):
    expo = jnp.exp(logp - jnp.max(logp, axis=0, keepdims=True))
    return expo / jnp.sum(expo, axis=0, keepdims=True)


def eliminate(cov):
    width = cov.shape[0]
    blocks = width // 8
    i = lax.broadcasted_iota(jnp.int32, (width, width), 0)
    j = lax.broadcasted_iota(jnp.int32, (width, width), 1)
    eye = (i == j).astype(jnp.float32)
    aug = jnp.concatenate([cov, eye], axis=1)
    rows = [aug[8 * b : 8 * b + 8, :] for b in range(blocks)]
    wide = (8, 2 * width)
    sub = lax.broadcasted_iota(jnp.int32, wide, 0)
    for b in range(blocks):
        cols = [
            [jnp.broadcast_to(rows[bb][:, 8 * b + k : 8 * b + k + 1], wide) for bb in range(b, blocks)]
            for k in range(8)
        ]
        for s in range(0, 8, 2):
            spread = [[jnp.broadcast_to(v[t : t + 1, :], wide) for t in (s, s + 1)] for v in [rows[b]] + [c[0] for c in cols]]
            (top, mid), low = spread[1 + s], spread[2 + s][1]
            inverse = 1.0 / (top * low - mid * mid)
            for n in range(blocks - b):
                one, two = cols[s][n], cols[s + 1][n]
                f = (one * low - two * mid) * inverse
                h = (two * top - one * mid) * inverse
                row_f = f
                if n == 0:
                    f = jnp.where(sub > s + 1, f, 0.0)
                    h = jnp.where(sub > s + 1, h, 0.0)
                    row_f = jnp.where(sub == s + 1, mid / top, f)
                for k in range(s + 2, 8):
                    cols[k][n] = cols[k][n] - (f * spread[1 + k][0] + h * spread[1 + k][1])
                rows[b + n] = rows[b + n] - (row_f * spread[0][0] + h * spread[0][1])
    full = jnp.concatenate(rows, axis=0)
    diag = jnp.sum(full[:, :width] * eye, axis=1, keepdims=True)
    return full * lax.rsqrt(diag), diag


def kernel(
    ng, nd, regimes, width, dl, pb,
    anom_hbm, eofs_ref, means_hbm, var_hbm, mix_hbm,
    o_means, o_covs, o_weights, o_member, o_comp,
    means_ref, var_ref, mix_ref, anom, eall, acc, pout, pin, dbuf, rbuf, qbuf, msend, msib, chip, mrecv, gslot, res, cres, memall, cacc, cout, cin, csend, crecv, cnt,
    anom_sem, e_send, e_fwd, e_recv, p_send, p_recv, s_send, s_recv, m_send, m_recv, g_send, g_recv,
    r_send, r_fwd, r_recv, c_send, c_fwd, c_recv, y_send, y_recv, u_send, u_recv, t_send, t_recv, n_send, n_recv, i_sem,
):
    g = lax.axis_index("grid")
    d = lax.axis_index("day")
    half = width // 2
    sibling = d + 1 - 2 * lax.rem(d, 2)
    nz = nd // 2
    pairs_of = regimes // 2
    core = lax.rem(d, 2)
    z = lax.div(d, 2)

    def day_peer(k):
        return lax.rem(d + k, nd)

    def grid_peer(k):
        return lax.rem(g + k, ng)

    offsets = []
    for k in range(1, nz // 2 + 1):
        offsets.append(k)
        if nz - k != k:
            offsets.append(nz - k)

    def block_pairs():
        pairs = [(d, sibling)]
        for o in offsets:
            same = lax.rem(d + 2 * o, nd)
            pairs.append((same, same + 1 - 2 * lax.rem(same, 2)))
        return pairs

    def load(s):
        return pltpu.make_async_copy(
            anom_hbm.at[:, pl.ds(pl.multiple_of(s * pb, pb), pb)], anom.at[s], anom_sem.at[s]
        )

    first_copies = [
        pltpu.make_async_copy(eofs_ref, eall.at[d], i_sem.at[0]),
        pltpu.make_async_copy(means_hbm, means_ref, i_sem.at[1]),
        pltpu.make_async_copy(var_hbm, var_ref, i_sem.at[2]),
        pltpu.make_async_copy(mix_hbm, mix_ref, i_sem.at[3]),
    ]
    for copy in first_copies:
        copy.start()
    places = list(range(pairs_of))
    if pairs_of == nz:
        places = [lax.rem(z + o, nz) for o in reversed(offsets)] + [z]
    pairs = block_pairs()
    for pair in pairs:
        for s in pair:
            load(s).start()

    barrier = pltpu.get_barrier_semaphore()
    for k in range(1, nd):
        pl.semaphore_signal(barrier, inc=1, device_id=(g, day_peer(k)), device_id_type=MESH)
    for k in range(1, ng):
        pl.semaphore_signal(barrier, inc=1, device_id=(grid_peer(k), d), device_id_type=MESH)
    pl.semaphore_wait(barrier, nd - 1 + ng - 1)

    def remote(src, dst, send, recv, target):
        return pltpu.make_async_remote_copy(
            src_ref=src, dst_ref=dst, send_sem=send, recv_sem=recv, device_id=target, device_id_type=MESH
        )

    sent = []

    near = [lax.rem(d + 2 * o, nd) for o in offsets] + [sibling]
    for n, target in enumerate(near):
        copy = remote(eofs_ref, eall.at[d], e_send.at[n], e_recv.at[d], (g, target))
        copy.start()
        sent.append(copy)

    def part(i):
        return pl.ds(pl.multiple_of(i * dl, dl), dl)

    count = 0
    for n, pair in enumerate(pairs):
        for m, s in enumerate(pair):
            if n == 0 and m == 0:
                first_copies[0].wait()
                block = eall[s]
            else:
                remote(eall.at[s], eall.at[s], e_send.at[0], e_recv.at[s], (g, sibling)).wait_recv()
                if m == 0:
                    copy = remote(eall.at[s], eall.at[s], e_fwd.at[n - 1], e_recv.at[s], (g, sibling))
                    copy.start()
                    sent.append(copy)
                block = eall[s]
            load(s).wait()
            count += 1
            if count < nd:
                term = lax.dot_general(anom[s], block, NT, preferred_element_type=jnp.float32)
                acc[...] = term if count == 1 else acc[...] + term
            else:
                for k in list(range(1, ng)) + [0]:
                    i = grid_peer(k)
                    term = lax.dot_general(anom[s, part(i), :], block, NT, preferred_element_type=jnp.float32)
                    total = (acc[part(i), :] + term).T
                    if k == 0:
                        pin[g] = total
                    else:
                        pout[i] = total
                        copy = remote(pout.at[i], pin.at[g], p_send.at[k - 1], p_recv.at[g], (i, d))
                        copy.start()
                        sent.append(copy)
    for k in range(1, ng):
        i = grid_peer(k)
        remote(pout.at[i], pin.at[i], p_send.at[k - 1], p_recv.at[i], (i, d)).wait_recv()
    x = pin[0]
    for i in range(1, ng):
        x = x + pin[i]

    for copy in first_copies[1:]:
        copy.wait()
    means = means_ref[...]
    variances = var_ref[...]
    er = lax.broadcasted_iota(jnp.int32, (regimes, regimes), 0)
    ec = lax.broadcasted_iota(jnp.int32, (regimes, regimes), 1)
    mix = jnp.sum(jnp.where(er == ec, mix_ref[...].reshape(1, regimes), 0.0), axis=1, keepdims=True)
    mcol = columns_of(means)
    scale = columns_of(lax.rsqrt(variances))
    logw = jnp.log(mix / jnp.sum(mix, axis=0, keepdims=True))
    logdet = 0.5 * jnp.sum(jnp.log(variances), axis=1, keepdims=True)
    quad = []
    for r in range(regimes):
        dbuf[r] = x - mcol[:, r : r + 1]
        y = dbuf[r] * scale[:, r : r + 1]
        quad.append(jnp.sum(y * y, axis=0, keepdims=True))
    resp = softmax_regimes(logw - logdet - 0.5 * jnp.concatenate(quad, axis=0))

    lane = lax.broadcasted_iota(jnp.int32, (8, width), 1)
    ei = lax.broadcasted_iota(jnp.int32, (width, width), 0)
    ej = lax.broadcasted_iota(jnp.int32, (width, width), 1)
    eye = (ei == ej).astype(jnp.float32)

    for it in range(ITERS):
        rbuf[...] = resp

        def moments(r):
            diff = dbuf[r]
            share = rbuf[pl.ds(r, 1), :]
            lhs = jnp.concatenate([diff * share, jnp.broadcast_to(share, (8, dl))], axis=0)
            out = lax.dot_general(lhs, diff, NT, precision=PRECISE, preferred_element_type=jnp.float32)
            number = jnp.broadcast_to(jnp.sum(share, axis=1, keepdims=True), (8, width))
            second = jnp.concatenate([out[0:half], out[half:width]], axis=1)
            return second, jnp.concatenate([out[width : width + 8], number], axis=1)

        for n in places:
            msend[it, n, 0:half, :], msend[it, n, half : half + 8, :] = moments(2 * n + 1 - core)
            remote(msend.at[it, n], msib.at[it, n], s_send.at[it, n], s_recv.at[it, n], (g, sibling)).start()
        for n in places:
            second, tail = moments(2 * n + core)
            remote(msib.at[it, n], msib.at[it, n], s_send.at[it, n], s_recv.at[it, n], (g, sibling)).wait_recv()
            chip[it, n, 0:half, :] = second + msib[it, n, 0:half, :]
            chip[it, n, half : half + 8, :] = tail + msib[it, n, half : half + 8, :]

            @pl.when(z != n)
            def _():
                remote(chip.at[it, n], mrecv.at[it, z], m_send.at[it, n], m_recv.at[it, z], (g, 2 * n + core)).start()

        def own():
            mrecv[it, z] = chip[it, z]
            for k in range(1, nz):
                s = lax.rem(z + k, nz)
                remote(mrecv.at[it, s], mrecv.at[it, s], m_send.at[it, 0], m_recv.at[it, s], (g, sibling)).wait_recv()
            total = mrecv[it, 0]
            for s in range(1, nz):
                total = total + mrecv[it, s]
            gslot[it, g] = total
            for k in range(1, ng):
                copy = remote(gslot.at[it, g], gslot.at[it, g], g_send.at[it, k - 1], g_recv.at[it, g], (grid_peer(k), d))
                copy.start()
            for k in range(1, ng):
                i = grid_peer(k)
                remote(gslot.at[it, i], gslot.at[it, i], g_send.at[it, 0], g_recv.at[it, i], (i, d)).wait_recv()
            total = gslot[it, 0]
            for i in range(1, ng):
                total = total + gslot[it, i]
            second = jnp.concatenate([total[0:half, 0:width], total[0:half, width : 2 * width]], axis=0)
            first = total[half : half + 1, 0:width]
            number = total[half : half + 1, width : 2 * width]
            counted = jnp.maximum(number, 1.0)
            old = means_ref[pl.ds(d, 1), :] if it == 0 else res[it - 1, d, half : half + 1, 0:width]
            delta = (first + (number - counted) * old) / counted
            new = old + delta
            pad = jnp.zeros((6, width), jnp.float32)
            cols = columns_of(jnp.concatenate([delta, first, pad], axis=0))
            dcol, fcol = cols[:, 0:1], cols[:, 1:2]
            moved = second - dcol * first - fcol * delta + dcol * (delta * number)
            cov = moved / counted + REG * eye
            factor, diag = eliminate(cov)
            hld = 0.5 * jnp.sum(jnp.log(diag), axis=0, keepdims=True)
            res[it, d, 0:half, :] = jnp.concatenate(
                [factor[0:half, width : 2 * width], factor[half:width, width : 2 * width]], axis=1
            )
            tail = jnp.where(lane < half, jnp.broadcast_to(counted, (8, width)), jnp.broadcast_to(hld, (8, width)))
            res[it, d, half : half + 8, :] = jnp.concatenate([jnp.broadcast_to(new, (8, width)), tail], axis=1)
            for n, target in enumerate(near):
                remote(res.at[it, d], res.at[it, d], r_send.at[it, n], r_recv.at[it, d], (g, target)).start()
            if it == ITERS - 1:
                cres[d] = jnp.concatenate([cov[0:half], cov[half:width]], axis=1)
                for n, target in enumerate(near):
                    remote(cres.at[d], cres.at[d], c_send.at[n], c_recv.at[d], (g, target)).start()

        if nd > regimes:
            pl.when(d < regimes)(own)
        else:
            own()

        def distance(r):
            mean = columns_of(res[it, r, half : half + 8, 0:width])[:, 0:1]
            folded = res[it, r, 0:half, :]
            factor = jnp.concatenate([folded[:, 0:width], folded[:, width : 2 * width]], axis=0)
            diff = x - mean
            dbuf[r] = diff
            y = jnp.dot(factor, diff, precision=PRECISE, preferred_element_type=jnp.float32)
            qbuf[pl.ds(r, 1), :] = jnp.sum(y * y, axis=0, keepdims=True)

        for n in reversed(places):
            r = 2 * n + core

            @pl.when(z != n)
            def _():
                copy = remote(res.at[it, r], res.at[it, r], r_fwd.at[it, n], r_recv.at[it, r], (g, sibling))
                copy.wait_recv()
                copy.start()

            distance(r)
        for n in reversed(places):
            r = 2 * n + 1 - core
            remote(res.at[it, r], res.at[it, r], r_fwd.at[it, n], r_recv.at[it, r], (g, sibling)).wait_recv()
            distance(r)

        means = jnp.concatenate([res[it, r, half : half + 1, 0:width] for r in range(regimes)], axis=0)
        tails = jnp.concatenate([res[it, r, half : half + 1, width : 2 * width] for r in range(regimes)], axis=0)
        counted = tails[:, 0:1]
        weights = counted / jnp.sum(counted, axis=0, keepdims=True)
        logp = jnp.log(weights) - tails[:, half : half + 1] - 0.5 * qbuf[...]
        resp = softmax_regimes(logp)

    memall[g] = resp
    for k in range(1, ng):
        copy = remote(memall.at[g], memall.at[g], y_send.at[k - 1], y_recv.at[g], (grid_peer(k), d))
        copy.start()
        sent.append(copy)
    mine = resp.astype(jnp.bfloat16)
    for s in range(nd):
        cacc[s] = jnp.dot(mine, anom[s, part(g), :], preferred_element_type=jnp.float32)
    o_means[...] = means
    o_weights[...] = jnp.sum(jnp.where(er == ec, weights, 0.0), axis=0)
    for k in range(1, ng):
        i = grid_peer(k)
        remote(memall.at[i], memall.at[i], y_send.at[0], y_recv.at[i], (i, d)).wait_recv()
    member = jnp.concatenate([memall[i] for i in range(ng)], axis=1)
    o_member[...] = member
    cnt[d] = jnp.broadcast_to(jnp.sum(member, axis=1, keepdims=True), (regimes, 128))
    for k in range(1, nd):
        copy = remote(cnt.at[d], cnt.at[d], n_send.at[k - 1], n_recv.at[d], (g, day_peer(k)))
        copy.start()
        sent.append(copy)

    def field_sums(s):
        def add(k, total):
            i = grid_peer(k)
            days = memall[i].astype(jnp.bfloat16)
            return total + jnp.dot(days, anom[s, part(i), :], preferred_element_type=jnp.float32)

        total = cacc[s]
        if ng > 4:
            return lax.fori_loop(1, ng, add, total)
        for k in range(1, ng):
            total = add(k, total)
        return total

    order = [lax.rem(z + o, nz) for o in reversed(offsets)] + [z]
    for n in order:
        cout[n] = field_sums(2 * n + 1 - core)
        copy = remote(cout.at[n], cin.at[n], u_send.at[n], u_recv.at[n], (g, sibling))
        copy.start()
        sent.append(copy)

    for n in range(pairs_of):
        r = 2 * n + core

        @pl.when(z != n)
        def _():
            copy = remote(cres.at[r], cres.at[r], c_fwd.at[n], c_recv.at[r], (g, sibling))
            copy.wait_recv()
            copy.start()

    for n in order:
        terms = field_sums(2 * n + core)
        remote(cin.at[n], cin.at[n], u_send.at[n], u_recv.at[n], (g, sibling)).wait_recv()
        terms = terms + cin[n]
        if n is z:
            crecv[z] = terms
        else:
            csend[n] = terms
            copy = remote(csend.at[n], crecv.at[z], t_send.at[n], t_recv.at[z], (g, 2 * n + core))
            copy.start()
            sent.append(copy)

    for n in range(pairs_of):
        r = 2 * n + 1 - core
        remote(cres.at[r], cres.at[r], c_fwd.at[n], c_recv.at[r], (g, sibling)).wait_recv()
    for r in range(regimes):
        folded = cres[r]
        o_covs[r, 0:half, :] = folded[:, 0:width]
        o_covs[r, half:width, :] = folded[:, width : 2 * width]

    for k in range(1, nd):
        s = day_peer(k)
        remote(cnt.at[s], cnt.at[s], n_send.at[0], n_recv.at[s], (g, s)).wait_recv()
    number = cnt[0]
    for s in range(1, nd):
        number = number + cnt[s]
    for n in order[:-1]:
        remote(crecv.at[n], crecv.at[n], t_send.at[n], t_recv.at[n], (g, sibling)).wait_recv()
    total = crecv[0]
    for n in range(1, nz):
        total = total + crecv[n]
    o_comp[...] = (total / jnp.maximum(number[:, 0:1], 1.0)).astype(jnp.bfloat16)

    for copy in sent:
        copy.wait_send()
    for it in range(ITERS):
        for n in range(pairs_of):
            r = 2 * n + core
            remote(msend.at[it, n], msib.at[it, n], s_send.at[it, n], s_recv.at[it, n], (g, sibling)).wait_send()

            @pl.when(z != n)
            def _():
                remote(chip.at[it, n], mrecv.at[it, z], m_send.at[it, n], m_recv.at[it, z], (g, r)).wait_send()
                remote(res.at[it, r], res.at[it, r], r_fwd.at[it, n], r_recv.at[it, r], (g, sibling)).wait_send()
                if it == ITERS - 1:
                    remote(cres.at[r], cres.at[r], c_fwd.at[n], c_recv.at[r], (g, sibling)).wait_send()

        def own_sent():
            for k in range(1, ng):
                remote(gslot.at[it, g], gslot.at[it, g], g_send.at[it, k - 1], g_recv.at[it, 0], (grid_peer(k), d)).wait_send()
            for n, target in enumerate(near):
                remote(res.at[it, d], res.at[it, d], r_send.at[it, n], r_recv.at[it, d], (g, target)).wait_send()
                if it == ITERS - 1:
                    remote(cres.at[d], cres.at[d], c_send.at[n], c_recv.at[d], (g, target)).wait_send()

        if nd > regimes:
            pl.when(d < regimes)(own_sent)
        else:
            own_sent()


def hand_over(*refs):
    n = len(refs) // 2
    for i in range(n):
        refs[n + i][...] = refs[i][...]


def solution(mesh):
    ng, nd = mesh.shape["grid"], mesh.shape["day"]

    def body(anomalies, eofs, means_init, variances, mixing):
        days, pixels = anomalies.shape
        width, pb = eofs.shape
        regimes = means_init.shape[0]
        dl = days // ng
        half = width // 2
        nz = nd // 2
        f32 = jnp.float32
        vmem = pl.BlockSpec(memory_space=pltpu.VMEM)
        dma = pltpu.SemaphoreType.DMA
        outs = pl.pallas_call(
            functools.partial(kernel, ng, nd, regimes, width, dl, pb),
            out_shape=(
                jax.ShapeDtypeStruct((regimes, width), f32),
                jax.ShapeDtypeStruct((regimes, width, width), f32),
                jax.ShapeDtypeStruct((regimes,), f32),
                jax.ShapeDtypeStruct((regimes, days), f32),
                jax.ShapeDtypeStruct((regimes, pb), jnp.bfloat16),
            ),
            in_specs=[pl.BlockSpec(memory_space=pltpu.HBM)] * 5,
            out_specs=(vmem,) * 5,
            scratch_shapes=[
                pltpu.VMEM((regimes, width), f32),
                pltpu.VMEM((regimes, width), f32),
                pltpu.VMEM((regimes,), f32),
                pltpu.VMEM((nd, days, pb), jnp.bfloat16),
                pltpu.VMEM((nd, width, pb), jnp.bfloat16),
                pltpu.VMEM((days, width), f32),
                pltpu.VMEM((ng, width, dl), f32),
                pltpu.VMEM((ng, width, dl), f32),
                pltpu.VMEM((regimes, width, dl), f32),
                pltpu.VMEM((regimes, dl), f32),
                pltpu.VMEM((regimes, dl), f32),
                pltpu.VMEM((ITERS, regimes // 2, half + 8, 2 * width), f32),
                pltpu.VMEM((ITERS, regimes // 2, half + 8, 2 * width), f32),
                pltpu.VMEM((ITERS, regimes // 2, half + 8, 2 * width), f32),
                pltpu.VMEM((ITERS, nz, half + 8, 2 * width), f32),
                pltpu.VMEM((ITERS, ng, half + 8, 2 * width), f32),
                pltpu.VMEM((ITERS, regimes, half + 8, 2 * width), f32),
                pltpu.VMEM((regimes, half, 2 * width), f32),
                pltpu.VMEM((ng, regimes, dl), f32),
                pltpu.VMEM((nd, regimes, pb), f32),
                pltpu.VMEM((nz, regimes, pb), f32),
                pltpu.VMEM((nz, regimes, pb), f32),
                pltpu.VMEM((nz, regimes, pb), f32),
                pltpu.VMEM((nz, regimes, pb), f32),
                pltpu.VMEM((nd, regimes, 128), f32),
                dma((nd,)),
                dma((nz,)),
                dma((nz,)),
                dma((nd,)),
                dma((ng,)),
                dma((ng,)),
                dma((ITERS, regimes // 2)),
                dma((ITERS, regimes // 2)),
                dma((ITERS, regimes // 2)),
                dma((ITERS, nz)),
                dma((ITERS, ng)),
                dma((ITERS, ng)),
                dma((ITERS, nz)),
                dma((ITERS, regimes // 2)),
                dma((ITERS, regimes)),
                dma((nz,)),
                dma((regimes // 2,)),
                dma((regimes,)),
                dma((ng,)),
                dma((ng,)),
                dma((nz,)),
                dma((nz,)),
                dma((nz,)),
                dma((nz,)),
                dma((nd,)),
                dma((nd,)),
                dma((4,)),
            ],
            compiler_params=pltpu.CompilerParams(
                collective_id=0, has_side_effects=True, vmem_limit_bytes=60 * 1024 * 1024
            ),
            name="regimes",
        )(anomalies, eofs, means_init, variances, mixing)
        return pl.pallas_call(
            hand_over,
            out_shape=tuple(jax.ShapeDtypeStruct(o.shape, o.dtype) for o in outs),
            in_specs=[vmem] * len(outs),
            out_specs=(vmem,) * len(outs),
            compiler_params=pltpu.CompilerParams(vmem_limit_bytes=60 * 1024 * 1024),
            name="hand_over",
        )(*outs)

    in_specs = (P("day", "grid"), P(None, ("grid", "day")), P(), P(), P())
    out_specs = (P(), P(), P(), P(None, "day"), P(None, ("grid", "day")))
    return jax.shard_map(body, mesh=mesh, in_specs=in_specs, out_specs=out_specs, check_vma=False)
```

```python
import functools

import jax
import jax.numpy as jnp
from jax import lax
from jax.experimental import pallas as pl
from jax.experimental.pallas import tpu as pltpu
from jax.sharding import PartitionSpec as P

ITERS = 2
REG = 0.01
MESH = pl.DeviceIdType.MESH
PRECISE = lax.Precision.HIGHEST
NT = (((1,), (1,)), ((), ()))


def columns_of(rows):
    width = rows.shape[1]
    i = lax.broadcasted_iota(jnp.int32, (width, width), 0)
    j = lax.broadcasted_iota(jnp.int32, (width, width), 1)
    eye = (i == j).astype(jnp.float32)
    return lax.dot_general(eye, rows, NT, precision=PRECISE, preferred_element_type=jnp.float32)


def softmax_regimes(logp):
    expo = jnp.exp(logp - jnp.max(logp, axis=0, keepdims=True))
    return expo / jnp.sum(expo, axis=0, keepdims=True)


def eliminate(cov):
    width = cov.shape[0]
    blocks = width // 8
    i = lax.broadcasted_iota(jnp.int32, (width, width), 0)
    j = lax.broadcasted_iota(jnp.int32, (width, width), 1)
    eye = (i == j).astype(jnp.float32)
    aug = jnp.concatenate([cov, eye], axis=1)
    rows = [aug[8 * b : 8 * b + 8, :] for b in range(blocks)]
    wide = (8, 2 * width)
    sub = lax.broadcasted_iota(jnp.int32, wide, 0)
    for b in range(blocks):
        cols = [
            [jnp.broadcast_to(rows[bb][:, 8 * b + k : 8 * b + k + 1], wide) for bb in range(b, blocks)]
            for k in range(8)
        ]
        for s in range(0, 8, 2):
            spread = [[jnp.broadcast_to(v[t : t + 1, :], wide) for t in (s, s + 1)] for v in [rows[b]] + [c[0] for c in cols]]
            (top, mid), low = spread[1 + s], spread[2 + s][1]
            inverse = 1.0 / (top * low - mid * mid)
            for n in range(blocks - b):
                one, two = cols[s][n], cols[s + 1][n]
                f = (one * low - two * mid) * inverse
                h = (two * top - one * mid) * inverse
                row_f = f
                if n == 0:
                    f = jnp.where(sub > s + 1, f, 0.0)
                    h = jnp.where(sub > s + 1, h, 0.0)
                    row_f = jnp.where(sub == s + 1, mid / top, f)
                for k in range(s + 2, 8):
                    cols[k][n] = cols[k][n] - (f * spread[1 + k][0] + h * spread[1 + k][1])
                rows[b + n] = rows[b + n] - (row_f * spread[0][0] + h * spread[0][1])
    full = jnp.concatenate(rows, axis=0)
    diag = jnp.sum(full[:, :width] * eye, axis=1, keepdims=True)
    return full * lax.rsqrt(diag), diag


def kernel(
    ng, nd, regimes, width, dl, pb,
    anom_hbm, eofs_ref, means_hbm, var_hbm, mix_hbm,
    o_means, o_covs, o_weights, o_member, o_comp,
    means_ref, var_ref, mix_ref, anom, eall, acc, pout, pin, dbuf, rbuf, qbuf, msend, msib, chip, mrecv, gslot, res, cres, memall, cacc, cout, cin, csend, crecv, cnt,
    anom_sem, e_send, e_fwd, e_recv, p_send, p_recv, s_send, s_recv, m_send, m_recv, g_send, g_recv,
    r_send, r_fwd, r_recv, c_send, c_fwd, c_recv, y_send, y_recv, u_send, u_recv, t_send, t_recv, n_send, n_recv, i_sem,
):
    g = lax.axis_index("grid")
    d = lax.axis_index("day")
    half = width // 2
    sibling = d + 1 - 2 * lax.rem(d, 2)
    nz = nd // 2
    pairs_of = regimes // 2
    core = lax.rem(d, 2)
    z = lax.div(d, 2)

    def day_peer(k):
        return lax.rem(d + k, nd)

    def grid_peer(k):
        return lax.rem(g + k, ng)

    offsets = []
    for k in range(1, nz // 2 + 1):
        offsets.append(k)
        if nz - k != k:
            offsets.append(nz - k)

    def block_pairs():
        pairs = [(d, sibling)]
        for o in offsets:
            same = lax.rem(d + 2 * o, nd)
            pairs.append((same, same + 1 - 2 * lax.rem(same, 2)))
        return pairs

    def load(s):
        return pltpu.make_async_copy(
            anom_hbm.at[:, pl.ds(pl.multiple_of(s * pb, pb), pb)], anom.at[s], anom_sem.at[s]
        )

    first_copies = [
        pltpu.make_async_copy(eofs_ref, eall.at[d], i_sem.at[0]),
        pltpu.make_async_copy(means_hbm, means_ref, i_sem.at[1]),
        pltpu.make_async_copy(var_hbm, var_ref, i_sem.at[2]),
        pltpu.make_async_copy(mix_hbm, mix_ref, i_sem.at[3]),
    ]
    for copy in first_copies:
        copy.start()
    places = list(range(pairs_of))
    if pairs_of == nz:
        places = [lax.rem(z + o, nz) for o in reversed(offsets)] + [z]
    pairs = block_pairs()
    for pair in pairs:
        for s in pair:
            load(s).start()

    barrier = pltpu.get_barrier_semaphore()
    for k in range(1, nd):
        pl.semaphore_signal(barrier, inc=1, device_id=(g, day_peer(k)), device_id_type=MESH)
    for k in range(1, ng):
        pl.semaphore_signal(barrier, inc=1, device_id=(grid_peer(k), d), device_id_type=MESH)
    pl.semaphore_wait(barrier, nd - 1 + ng - 1)

    def remote(src, dst, send, recv, target):
        return pltpu.make_async_remote_copy(
            src_ref=src, dst_ref=dst, send_sem=send, recv_sem=recv, device_id=target, device_id_type=MESH
        )

    sent = []

    near = [lax.rem(d + 2 * o, nd) for o in offsets] + [sibling]
    for n, target in enumerate(near):
        copy = remote(eofs_ref, eall.at[d], e_send.at[n], e_recv.at[d], (g, target))
        copy.start()
        sent.append(copy)

    def part(i):
        return pl.ds(pl.multiple_of(i * dl, dl), dl)

    count = 0
    for n, pair in enumerate(pairs):
        for m, s in enumerate(pair):
            if n == 0 and m == 0:
                first_copies[0].wait()
                block = eall[s]
            else:
                remote(eall.at[s], eall.at[s], e_send.at[0], e_recv.at[s], (g, sibling)).wait_recv()
                if m == 0:
                    copy = remote(eall.at[s], eall.at[s], e_fwd.at[n - 1], e_recv.at[s], (g, sibling))
                    copy.start()
                    sent.append(copy)
                block = eall[s]
            load(s).wait()
            count += 1
            if count < nd:
                term = lax.dot_general(anom[s], block, NT, preferred_element_type=jnp.float32)
                acc[...] = term if count == 1 else acc[...] + term
            else:
                for k in list(range(1, ng)) + [0]:
                    i = grid_peer(k)
                    term = lax.dot_general(anom[s, part(i), :], block, NT, preferred_element_type=jnp.float32)
                    total = (acc[part(i), :] + term).T
                    if k == 0:
                        pin[g] = total
                    else:
                        pout[i] = total
                        copy = remote(pout.at[i], pin.at[g], p_send.at[k - 1], p_recv.at[g], (i, d))
                        copy.start()
                        sent.append(copy)
    for k in range(1, ng):
        i = grid_peer(k)
        remote(pout.at[i], pin.at[i], p_send.at[k - 1], p_recv.at[i], (i, d)).wait_recv()
    x = pin[0]
    for i in range(1, ng):
        x = x + pin[i]

    for copy in first_copies[1:]:
        copy.wait()
    means = means_ref[...]
    variances = var_ref[...]
    er = lax.broadcasted_iota(jnp.int32, (regimes, regimes), 0)
    ec = lax.broadcasted_iota(jnp.int32, (regimes, regimes), 1)
    mix = jnp.sum(jnp.where(er == ec, mix_ref[...].reshape(1, regimes), 0.0), axis=1, keepdims=True)
    mcol = columns_of(means)
    scale = columns_of(lax.rsqrt(variances))
    logw = jnp.log(mix / jnp.sum(mix, axis=0, keepdims=True))
    logdet = 0.5 * jnp.sum(jnp.log(variances), axis=1, keepdims=True)
    quad = []
    for r in range(regimes):
        dbuf[r] = x - mcol[:, r : r + 1]
        y = dbuf[r] * scale[:, r : r + 1]
        quad.append(jnp.sum(y * y, axis=0, keepdims=True))
    resp = softmax_regimes(logw - logdet - 0.5 * jnp.concatenate(quad, axis=0))

    lane = lax.broadcasted_iota(jnp.int32, (8, width), 1)
    ei = lax.broadcasted_iota(jnp.int32, (width, width), 0)
    ej = lax.broadcasted_iota(jnp.int32, (width, width), 1)
    eye = (ei == ej).astype(jnp.float32)

    for it in range(ITERS):
        rbuf[...] = resp

        def moments(r):
            diff = dbuf[r]
            share = rbuf[pl.ds(r, 1), :]
            lhs = jnp.concatenate([diff * share, jnp.broadcast_to(share, (8, dl))], axis=0)
            out = lax.dot_general(lhs, diff, NT, precision=PRECISE, preferred_element_type=jnp.float32)
            number = jnp.broadcast_to(jnp.sum(share, axis=1, keepdims=True), (8, width))
            second = jnp.concatenate([out[0:half], out[half:width]], axis=1)
            return second, jnp.concatenate([out[width : width + 8], number], axis=1)

        for n in places:
            msend[it, n, 0:half, :], msend[it, n, half : half + 8, :] = moments(2 * n + 1 - core)
        for n in places:
            remote(msend.at[it, n], msib.at[it, n], s_send.at[it, n], s_recv.at[it, n], (g, sibling)).start()
        for n in places:
            chip[it, n, 0:half, :], chip[it, n, half : half + 8, :] = moments(2 * n + core)
        for n in places:
            remote(msib.at[it, n], msib.at[it, n], s_send.at[it, n], s_recv.at[it, n], (g, sibling)).wait_recv()
            chip[it, n] = chip[it, n] + msib[it, n]

            @pl.when(z != n)
            def _():
                remote(chip.at[it, n], mrecv.at[it, z], m_send.at[it, n], m_recv.at[it, z], (g, 2 * n + core)).start()

        def own():
            mrecv[it, z] = chip[it, z]
            for k in range(1, nz):
                s = lax.rem(z + k, nz)
                remote(mrecv.at[it, s], mrecv.at[it, s], m_send.at[it, 0], m_recv.at[it, s], (g, sibling)).wait_recv()
            total = mrecv[it, 0]
            for s in range(1, nz):
                total = total + mrecv[it, s]
            gslot[it, g] = total
            for k in range(1, ng):
                copy = remote(gslot.at[it, g], gslot.at[it, g], g_send.at[it, k - 1], g_recv.at[it, g], (grid_peer(k), d))
                copy.start()
            for k in range(1, ng):
                i = grid_peer(k)
                remote(gslot.at[it, i], gslot.at[it, i], g_send.at[it, 0], g_recv.at[it, i], (i, d)).wait_recv()
            total = gslot[it, 0]
            for i in range(1, ng):
                total = total + gslot[it, i]
            second = jnp.concatenate([total[0:half, 0:width], total[0:half, width : 2 * width]], axis=0)
            first = total[half : half + 1, 0:width]
            number = total[half : half + 1, width : 2 * width]
            counted = jnp.maximum(number, 1.0)
            old = means_ref[pl.ds(d, 1), :] if it == 0 else res[it - 1, d, half : half + 1, 0:width]
            delta = (first + (number - counted) * old) / counted
            new = old + delta
            pad = jnp.zeros((6, width), jnp.float32)
            cols = columns_of(jnp.concatenate([delta, first, pad], axis=0))
            dcol, fcol = cols[:, 0:1], cols[:, 1:2]
            moved = second - dcol * first - fcol * delta + dcol * (delta * number)
            cov = moved / counted + REG * eye
            factor, diag = eliminate(cov)
            hld = 0.5 * jnp.sum(jnp.log(diag), axis=0, keepdims=True)
            res[it, d, 0:half, :] = jnp.concatenate(
                [factor[0:half, width : 2 * width], factor[half:width, width : 2 * width]], axis=1
            )
            tail = jnp.where(lane < half, jnp.broadcast_to(counted, (8, width)), jnp.broadcast_to(hld, (8, width)))
            res[it, d, half : half + 8, :] = jnp.concatenate([jnp.broadcast_to(new, (8, width)), tail], axis=1)
            for n, target in enumerate(near):
                remote(res.at[it, d], res.at[it, d], r_send.at[it, n], r_recv.at[it, d], (g, target)).start()
            if it == ITERS - 1:
                cres[d] = jnp.concatenate([cov[0:half], cov[half:width]], axis=1)
                for n, target in enumerate(near):
                    remote(cres.at[d], cres.at[d], c_send.at[n], c_recv.at[d], (g, target)).start()

        if nd > regimes:
            pl.when(d < regimes)(own)
        else:
            own()

        def distances(batch):
            centres = [res[it, r, half : half + 1, 0:width] for r in batch]
            centres = columns_of(jnp.concatenate(centres + centres[: -len(batch) % 8], axis=0))
            for n, r in enumerate(batch):
                folded = res[it, r, 0:half, :]
                factor = jnp.concatenate([folded[:, 0:width], folded[:, width : 2 * width]], axis=0)
                diff = x - centres[:, n : n + 1]
                dbuf[r] = diff
                y = jnp.dot(factor, diff, precision=PRECISE, preferred_element_type=jnp.float32)
                qbuf[pl.ds(r, 1), :] = jnp.sum(y * y, axis=0, keepdims=True)

        for n in reversed(places):
            r = 2 * n + core

            @pl.when(z != n)
            def _():
                copy = remote(res.at[it, r], res.at[it, r], r_fwd.at[it, n], r_recv.at[it, r], (g, sibling))
                copy.wait_recv()
                copy.start()

        distances([2 * n + core for n in reversed(places)])
        for n in reversed(places):
            r = 2 * n + 1 - core
            remote(res.at[it, r], res.at[it, r], r_fwd.at[it, n], r_recv.at[it, r], (g, sibling)).wait_recv()
        distances([2 * n + 1 - core for n in reversed(places)])

        means = jnp.concatenate([res[it, r, half : half + 1, 0:width] for r in range(regimes)], axis=0)
        tails = jnp.concatenate([res[it, r, half : half + 1, width : 2 * width] for r in range(regimes)], axis=0)
        counted = tails[:, 0:1]
        weights = counted / jnp.sum(counted, axis=0, keepdims=True)
        logp = jnp.log(weights) - tails[:, half : half + 1] - 0.5 * qbuf[...]
        resp = softmax_regimes(logp)

    memall[g] = resp
    for k in range(1, ng):
        copy = remote(memall.at[g], memall.at[g], y_send.at[k - 1], y_recv.at[g], (grid_peer(k), d))
        copy.start()
        sent.append(copy)
    mine = resp.astype(jnp.bfloat16)
    for s in range(nd):
        cacc[s] = jnp.dot(mine, anom[s, part(g), :], preferred_element_type=jnp.float32)
    o_means[...] = means
    o_weights[...] = jnp.sum(jnp.where(er == ec, weights, 0.0), axis=0)
    for k in range(1, ng):
        i = grid_peer(k)
        remote(memall.at[i], memall.at[i], y_send.at[0], y_recv.at[i], (i, d)).wait_recv()
    member = jnp.concatenate([memall[i] for i in range(ng)], axis=1)
    o_member[...] = member
    cnt[d] = jnp.broadcast_to(jnp.sum(member, axis=1, keepdims=True), (regimes, 128))
    for k in range(1, nd):
        copy = remote(cnt.at[d], cnt.at[d], n_send.at[k - 1], n_recv.at[d], (g, day_peer(k)))
        copy.start()
        sent.append(copy)

    def field_sums(s):
        def add(k, total):
            i = grid_peer(k)
            days = memall[i].astype(jnp.bfloat16)
            return total + jnp.dot(days, anom[s, part(i), :], preferred_element_type=jnp.float32)

        total = cacc[s]
        if ng > 4:
            return lax.fori_loop(1, ng, add, total)
        for k in range(1, ng):
            total = add(k, total)
        return total

    order = [lax.rem(z + o, nz) for o in reversed(offsets)] + [z]
    for n in order:
        cout[n] = field_sums(2 * n + 1 - core)
        copy = remote(cout.at[n], cin.at[n], u_send.at[n], u_recv.at[n], (g, sibling))
        copy.start()
        sent.append(copy)

    for n in range(pairs_of):
        r = 2 * n + core

        @pl.when(z != n)
        def _():
            copy = remote(cres.at[r], cres.at[r], c_fwd.at[n], c_recv.at[r], (g, sibling))
            copy.wait_recv()
            copy.start()

    for n in order:
        terms = field_sums(2 * n + core)
        remote(cin.at[n], cin.at[n], u_send.at[n], u_recv.at[n], (g, sibling)).wait_recv()
        terms = terms + cin[n]
        if n is z:
            crecv[z] = terms
        else:
            csend[n] = terms
            copy = remote(csend.at[n], crecv.at[z], t_send.at[n], t_recv.at[z], (g, 2 * n + core))
            copy.start()
            sent.append(copy)

    for n in range(pairs_of):
        r = 2 * n + 1 - core
        remote(cres.at[r], cres.at[r], c_fwd.at[n], c_recv.at[r], (g, sibling)).wait_recv()
    for r in range(regimes):
        folded = cres[r]
        o_covs[r, 0:half, :] = folded[:, 0:width]
        o_covs[r, half:width, :] = folded[:, width : 2 * width]

    for k in range(1, nd):
        s = day_peer(k)
        remote(cnt.at[s], cnt.at[s], n_send.at[0], n_recv.at[s], (g, s)).wait_recv()
    number = cnt[0]
    for s in range(1, nd):
        number = number + cnt[s]
    for n in order[:-1]:
        remote(crecv.at[n], crecv.at[n], t_send.at[n], t_recv.at[n], (g, sibling)).wait_recv()
    total = crecv[0]
    for n in range(1, nz):
        total = total + crecv[n]
    o_comp[...] = (total / jnp.maximum(number[:, 0:1], 1.0)).astype(jnp.bfloat16)

    for copy in sent:
        copy.wait_send()
    for it in range(ITERS):
        for n in range(pairs_of):
            r = 2 * n + core
            remote(msend.at[it, n], msib.at[it, n], s_send.at[it, n], s_recv.at[it, n], (g, sibling)).wait_send()

            @pl.when(z != n)
            def _():
                remote(chip.at[it, n], mrecv.at[it, z], m_send.at[it, n], m_recv.at[it, z], (g, r)).wait_send()
                remote(res.at[it, r], res.at[it, r], r_fwd.at[it, n], r_recv.at[it, r], (g, sibling)).wait_send()
                if it == ITERS - 1:
                    remote(cres.at[r], cres.at[r], c_fwd.at[n], c_recv.at[r], (g, sibling)).wait_send()

        def own_sent():
            for k in range(1, ng):
                remote(gslot.at[it, g], gslot.at[it, g], g_send.at[it, k - 1], g_recv.at[it, 0], (grid_peer(k), d)).wait_send()
            for n, target in enumerate(near):
                remote(res.at[it, d], res.at[it, d], r_send.at[it, n], r_recv.at[it, d], (g, target)).wait_send()
                if it == ITERS - 1:
                    remote(cres.at[d], cres.at[d], c_send.at[n], c_recv.at[d], (g, target)).wait_send()

        if nd > regimes:
            pl.when(d < regimes)(own_sent)
        else:
            own_sent()


def hand_over(*refs):
    n = len(refs) // 2
    for i in range(n):
        refs[n + i][...] = refs[i][...]


def solution(mesh):
    ng, nd = mesh.shape["grid"], mesh.shape["day"]

    def body(anomalies, eofs, means_init, variances, mixing):
        days, pixels = anomalies.shape
        width, pb = eofs.shape
        regimes = means_init.shape[0]
        dl = days // ng
        half = width // 2
        nz = nd // 2
        f32 = jnp.float32
        vmem = pl.BlockSpec(memory_space=pltpu.VMEM)
        dma = pltpu.SemaphoreType.DMA
        outs = pl.pallas_call(
            functools.partial(kernel, ng, nd, regimes, width, dl, pb),
            out_shape=(
                jax.ShapeDtypeStruct((regimes, width), f32),
                jax.ShapeDtypeStruct((regimes, width, width), f32),
                jax.ShapeDtypeStruct((regimes,), f32),
                jax.ShapeDtypeStruct((regimes, days), f32),
                jax.ShapeDtypeStruct((regimes, pb), jnp.bfloat16),
            ),
            in_specs=[pl.BlockSpec(memory_space=pltpu.HBM)] * 5,
            out_specs=(vmem,) * 5,
            scratch_shapes=[
                pltpu.VMEM((regimes, width), f32),
                pltpu.VMEM((regimes, width), f32),
                pltpu.VMEM((regimes,), f32),
                pltpu.VMEM((nd, days, pb), jnp.bfloat16),
                pltpu.VMEM((nd, width, pb), jnp.bfloat16),
                pltpu.VMEM((days, width), f32),
                pltpu.VMEM((ng, width, dl), f32),
                pltpu.VMEM((ng, width, dl), f32),
                pltpu.VMEM((regimes, width, dl), f32),
                pltpu.VMEM((regimes, dl), f32),
                pltpu.VMEM((regimes, dl), f32),
                pltpu.VMEM((ITERS, regimes // 2, half + 8, 2 * width), f32),
                pltpu.VMEM((ITERS, regimes // 2, half + 8, 2 * width), f32),
                pltpu.VMEM((ITERS, regimes // 2, half + 8, 2 * width), f32),
                pltpu.VMEM((ITERS, nz, half + 8, 2 * width), f32),
                pltpu.VMEM((ITERS, ng, half + 8, 2 * width), f32),
                pltpu.VMEM((ITERS, regimes, half + 8, 2 * width), f32),
                pltpu.VMEM((regimes, half, 2 * width), f32),
                pltpu.VMEM((ng, regimes, dl), f32),
                pltpu.VMEM((nd, regimes, pb), f32),
                pltpu.VMEM((nz, regimes, pb), f32),
                pltpu.VMEM((nz, regimes, pb), f32),
                pltpu.VMEM((nz, regimes, pb), f32),
                pltpu.VMEM((nz, regimes, pb), f32),
                pltpu.VMEM((nd, regimes, 128), f32),
                dma((nd,)),
                dma((nz,)),
                dma((nz,)),
                dma((nd,)),
                dma((ng,)),
                dma((ng,)),
                dma((ITERS, regimes // 2)),
                dma((ITERS, regimes // 2)),
                dma((ITERS, regimes // 2)),
                dma((ITERS, nz)),
                dma((ITERS, ng)),
                dma((ITERS, ng)),
                dma((ITERS, nz)),
                dma((ITERS, regimes // 2)),
                dma((ITERS, regimes)),
                dma((nz,)),
                dma((regimes // 2,)),
                dma((regimes,)),
                dma((ng,)),
                dma((ng,)),
                dma((nz,)),
                dma((nz,)),
                dma((nz,)),
                dma((nz,)),
                dma((nd,)),
                dma((nd,)),
                dma((4,)),
            ],
            compiler_params=pltpu.CompilerParams(
                collective_id=0, has_side_effects=True, vmem_limit_bytes=60 * 1024 * 1024
            ),
            name="regimes",
        )(anomalies, eofs, means_init, variances, mixing)
        return pl.pallas_call(
            hand_over,
            out_shape=tuple(jax.ShapeDtypeStruct(o.shape, o.dtype) for o in outs),
            in_specs=[vmem] * len(outs),
            out_specs=(vmem,) * len(outs),
            compiler_params=pltpu.CompilerParams(vmem_limit_bytes=60 * 1024 * 1024),
            name="hand_over",
        )(*outs)

    in_specs = (P("day", "grid"), P(None, ("grid", "day")), P(), P(), P())
    out_specs = (P(), P(), P(), P(None, "day"), P(None, ("grid", "day")))
    return jax.shard_map(body, mesh=mesh, in_specs=in_specs, out_specs=out_specs, check_vma=False)
```

```python
import functools

import jax
import jax.numpy as jnp
from jax import lax
from jax.experimental import pallas as pl
from jax.experimental.pallas import tpu as pltpu
from jax.sharding import PartitionSpec as P

ITERS = 2
REG = 0.01
MESH = pl.DeviceIdType.MESH
PRECISE = lax.Precision.HIGHEST
NT = (((1,), (1,)), ((), ()))


def columns_of(rows):
    width = rows.shape[1]
    i = lax.broadcasted_iota(jnp.int32, (width, width), 0)
    j = lax.broadcasted_iota(jnp.int32, (width, width), 1)
    eye = (i == j).astype(jnp.float32)
    return lax.dot_general(eye, rows, NT, precision=PRECISE, preferred_element_type=jnp.float32)


def softmax_regimes(logp):
    expo = jnp.exp(logp - jnp.max(logp, axis=0, keepdims=True))
    return expo / jnp.sum(expo, axis=0, keepdims=True)


def eliminate(cov):
    width = cov.shape[0]
    blocks = width // 8
    i = lax.broadcasted_iota(jnp.int32, (width, width), 0)
    j = lax.broadcasted_iota(jnp.int32, (width, width), 1)
    eye = (i == j).astype(jnp.float32)
    aug = jnp.concatenate([cov, eye], axis=1)
    rows = [aug[8 * b : 8 * b + 8, :] for b in range(blocks)]
    wide = (8, 2 * width)
    sub = lax.broadcasted_iota(jnp.int32, wide, 0)
    for b in range(blocks):
        cols = [
            [jnp.broadcast_to(rows[bb][:, 8 * b + k : 8 * b + k + 1], wide) for bb in range(b, blocks)]
            for k in range(8)
        ]
        for s in range(8):
            inverse = 1.0 / jnp.broadcast_to(cols[s][0][s : s + 1, :], wide)
            pivot_row = jnp.broadcast_to(rows[b][s : s + 1, :], wide)
            later = [jnp.broadcast_to(cols[k][0][s : s + 1, :], wide) for k in range(s + 1, 8)]
            for n in range(blocks - b):
                column = cols[s][n]
                if n == 0:
                    column = jnp.where(sub > s, column, 0.0)
                factor = column * inverse
                for k in range(s + 1, 8):
                    cols[k][n] = cols[k][n] - factor * later[k - s - 1]
                rows[b + n] = rows[b + n] - factor * pivot_row
    full = jnp.concatenate(rows, axis=0)
    diag = jnp.sum(full[:, :width] * eye, axis=1, keepdims=True)
    return full * lax.rsqrt(diag), diag


def kernel(
    ng, nd, regimes, width, dl, pb,
    anom_hbm, eofs_ref, means_hbm, var_hbm, mix_hbm,
    o_means, o_covs, o_weights, o_member, o_comp,
    means_ref, var_ref, mix_ref, anom, eall, acc, pout, pin, msend, msib, chip, mrecv, gslot, res, cres, memall, cacc, cout, cin, csend, crecv, cnt,
    anom_sem, e_send, e_fwd, e_recv, p_send, p_recv, s_send, s_recv, m_send, m_recv, g_send, g_recv,
    r_send, r_fwd, r_recv, c_send, c_fwd, c_recv, y_send, y_recv, u_send, u_recv, t_send, t_recv, n_send, n_recv, i_sem,
):
    g = lax.axis_index("grid")
    d = lax.axis_index("day")
    half = width // 2
    sibling = d + 1 - 2 * lax.rem(d, 2)
    nz = nd // 2
    pairs_of = regimes // 2
    core = lax.rem(d, 2)
    z = lax.div(d, 2)

    def day_peer(k):
        return lax.rem(d + k, nd)

    def grid_peer(k):
        return lax.rem(g + k, ng)

    offsets = []
    for k in range(1, nz // 2 + 1):
        offsets.append(k)
        if nz - k != k:
            offsets.append(nz - k)

    def block_pairs():
        pairs = [(d, sibling)]
        for o in offsets:
            same = lax.rem(d + 2 * o, nd)
            pairs.append((same, same + 1 - 2 * lax.rem(same, 2)))
        return pairs

    def load(s):
        return pltpu.make_async_copy(
            anom_hbm.at[:, pl.ds(pl.multiple_of(s * pb, pb), pb)], anom.at[s], anom_sem.at[s]
        )

    first_copies = [
        pltpu.make_async_copy(eofs_ref, eall.at[d], i_sem.at[0]),
        pltpu.make_async_copy(means_hbm, means_ref, i_sem.at[1]),
        pltpu.make_async_copy(var_hbm, var_ref, i_sem.at[2]),
        pltpu.make_async_copy(mix_hbm, mix_ref, i_sem.at[3]),
    ]
    for copy in first_copies:
        copy.start()
    pairs = block_pairs()
    for pair in pairs:
        for s in pair:
            load(s).start()

    barrier = pltpu.get_barrier_semaphore()
    for k in range(1, nd):
        pl.semaphore_signal(barrier, inc=1, device_id=(g, day_peer(k)), device_id_type=MESH)
    for k in range(1, ng):
        pl.semaphore_signal(barrier, inc=1, device_id=(grid_peer(k), d), device_id_type=MESH)
    pl.semaphore_wait(barrier, nd - 1 + ng - 1)

    def remote(src, dst, send, recv, target):
        return pltpu.make_async_remote_copy(
            src_ref=src, dst_ref=dst, send_sem=send, recv_sem=recv, device_id=target, device_id_type=MESH
        )

    sent = []

    near = [lax.rem(d + 2 * o, nd) for o in offsets] + [sibling]
    for n, target in enumerate(near):
        copy = remote(eofs_ref, eall.at[d], e_send.at[n], e_recv.at[d], (g, target))
        copy.start()
        sent.append(copy)

    def part(i):
        return pl.ds(pl.multiple_of(i * dl, dl), dl)

    count = 0
    for n, pair in enumerate(pairs):
        for m, s in enumerate(pair):
            if n == 0 and m == 0:
                first_copies[0].wait()
                block = eall[s]
            else:
                remote(eall.at[s], eall.at[s], e_send.at[0], e_recv.at[s], (g, sibling)).wait_recv()
                if m == 0:
                    copy = remote(eall.at[s], eall.at[s], e_fwd.at[n - 1], e_recv.at[s], (g, sibling))
                    copy.start()
                    sent.append(copy)
                block = eall[s]
            load(s).wait()
            count += 1
            if count < nd:
                term = lax.dot_general(anom[s], block, NT, preferred_element_type=jnp.float32)
                acc[...] = term if count == 1 else acc[...] + term
            else:
                for k in list(range(1, ng)) + [0]:
                    i = grid_peer(k)
                    term = lax.dot_general(anom[s, part(i), :], block, NT, preferred_element_type=jnp.float32)
                    total = (acc[part(i), :] + term).T
                    if k == 0:
                        pin[g] = total
                    else:
                        pout[i] = total
                        copy = remote(pout.at[i], pin.at[g], p_send.at[k - 1], p_recv.at[g], (i, d))
                        copy.start()
                        sent.append(copy)
    for k in range(1, ng):
        i = grid_peer(k)
        remote(pout.at[i], pin.at[i], p_send.at[k - 1], p_recv.at[i], (i, d)).wait_recv()
    x = pin[0]
    for i in range(1, ng):
        x = x + pin[i]

    for copy in first_copies[1:]:
        copy.wait()
    means = means_ref[...]
    variances = var_ref[...]
    er = lax.broadcasted_iota(jnp.int32, (regimes, regimes), 0)
    ec = lax.broadcasted_iota(jnp.int32, (regimes, regimes), 1)
    mix = jnp.sum(jnp.where(er == ec, mix_ref[...].reshape(1, regimes), 0.0), axis=1, keepdims=True)
    mcol = columns_of(means)
    scale = columns_of(lax.rsqrt(variances))
    logw = jnp.log(mix / jnp.sum(mix, axis=0, keepdims=True))
    logdet = 0.5 * jnp.sum(jnp.log(variances), axis=1, keepdims=True)
    quad = []
    for r in range(regimes):
        y = (x - mcol[:, r : r + 1]) * scale[:, r : r + 1]
        quad.append(jnp.sum(y * y, axis=0, keepdims=True))
    resp = softmax_regimes(logw - logdet - 0.5 * jnp.concatenate(quad, axis=0))

    lane = lax.broadcasted_iota(jnp.int32, (8, width), 1)
    ei = lax.broadcasted_iota(jnp.int32, (width, width), 0)
    ej = lax.broadcasted_iota(jnp.int32, (width, width), 1)
    eye = (ei == ej).astype(jnp.float32)

    for it in range(ITERS):
        counts = jnp.sum(resp, axis=1, keepdims=True)
        for r in range(regimes):
            diff = x - mcol[:, r : r + 1]
            lhs = jnp.concatenate([diff * resp[r : r + 1, :], resp], axis=0)
            out = lax.dot_general(lhs, diff, NT, precision=PRECISE, preferred_element_type=jnp.float32)
            msend[it, r, 0:half, :] = jnp.concatenate([out[0:half], out[half:width]], axis=1)
            first = jnp.broadcast_to(out[width + r : width + r + 1, :], (8, width))
            number = jnp.broadcast_to(counts[r : r + 1, :], (8, width))
            msend[it, r, half : half + 8, :] = jnp.concatenate([first, number], axis=1)

        for r in range(regimes):
            @pl.when(core != r % 2)
            def _():
                remote(msend.at[it, r], msib.at[it, r // 2], s_send.at[it, r // 2], s_recv.at[it, r // 2], (g, sibling)).start()

        for n in range(pairs_of):
            mine = 2 * n + core
            remote(msib.at[it, n], msib.at[it, n], s_send.at[it, n], s_recv.at[it, n], (g, sibling)).wait_recv()
            chip[it, n] = msend[it, mine] + msib[it, n]

            @pl.when(z != n)
            def _():
                remote(chip.at[it, n], mrecv.at[it, z], m_send.at[it, n], m_recv.at[it, z], (g, mine)).start()

        def own():
            mrecv[it, z] = chip[it, z]
            for k in range(1, nz):
                s = lax.rem(z + k, nz)
                remote(mrecv.at[it, s], mrecv.at[it, s], m_send.at[it, 0], m_recv.at[it, s], (g, sibling)).wait_recv()
            total = mrecv[it, 0]
            for s in range(1, nz):
                total = total + mrecv[it, s]
            gslot[it, g] = total
            for k in range(1, ng):
                copy = remote(gslot.at[it, g], gslot.at[it, g], g_send.at[it, k - 1], g_recv.at[it, g], (grid_peer(k), d))
                copy.start()
            for k in range(1, ng):
                i = grid_peer(k)
                remote(gslot.at[it, i], gslot.at[it, i], g_send.at[it, 0], g_recv.at[it, i], (i, d)).wait_recv()
            total = gslot[it, 0]
            for i in range(1, ng):
                total = total + gslot[it, i]
            second = jnp.concatenate([total[0:half, 0:width], total[0:half, width : 2 * width]], axis=0)
            first = total[half : half + 1, 0:width]
            number = total[half : half + 1, width : 2 * width]
            counted = jnp.maximum(number, 1.0)
            old = means_ref[pl.ds(d, 1), :] if it == 0 else res[it - 1, d, half : half + 1, 0:width]
            delta = (first + (number - counted) * old) / counted
            new = old + delta
            pad = jnp.zeros((6, width), jnp.float32)
            cols = columns_of(jnp.concatenate([delta, first, pad], axis=0))
            dcol, fcol = cols[:, 0:1], cols[:, 1:2]
            moved = second - dcol * first - fcol * delta + dcol * (delta * number)
            cov = moved / counted + REG * eye
            factor, diag = eliminate(cov)
            hld = 0.5 * jnp.sum(jnp.log(diag), axis=0, keepdims=True)
            res[it, d, 0:half, :] = jnp.concatenate(
                [factor[0:half, width : 2 * width], factor[half:width, width : 2 * width]], axis=1
            )
            tail = jnp.where(lane < half, jnp.broadcast_to(counted, (8, width)), jnp.broadcast_to(hld, (8, width)))
            res[it, d, half : half + 8, :] = jnp.concatenate([jnp.broadcast_to(new, (8, width)), tail], axis=1)
            for n, target in enumerate(near):
                remote(res.at[it, d], res.at[it, d], r_send.at[it, n], r_recv.at[it, d], (g, target)).start()
            if it == ITERS - 1:
                cres[d] = jnp.concatenate([cov[0:half], cov[half:width]], axis=1)
                for n, target in enumerate(near):
                    remote(cres.at[d], cres.at[d], c_send.at[n], c_recv.at[d], (g, target)).start()

        if nd > regimes:
            pl.when(d < regimes)(own)
        else:
            own()

        for n in range(pairs_of):
            r = 2 * n + core

            @pl.when(z != n)
            def _():
                copy = remote(res.at[it, r], res.at[it, r], r_fwd.at[it, n], r_recv.at[it, r], (g, sibling))
                copy.wait_recv()
                copy.start()

        for n in range(pairs_of):
            r = 2 * n + 1 - core
            remote(res.at[it, r], res.at[it, r], r_fwd.at[it, n], r_recv.at[it, r], (g, sibling)).wait_recv()

        means = jnp.concatenate([res[it, r, half : half + 1, 0:width] for r in range(regimes)], axis=0)
        tails = jnp.concatenate([res[it, r, half : half + 1, width : 2 * width] for r in range(regimes)], axis=0)
        counted = tails[:, 0:1]
        weights = counted / jnp.sum(counted, axis=0, keepdims=True)
        mcol = columns_of(means)
        quad = []
        for r in range(regimes):
            folded = res[it, r, 0:half, :]
            factor = jnp.concatenate([folded[:, 0:width], folded[:, width : 2 * width]], axis=0)
            y = jnp.dot(factor, x - mcol[:, r : r + 1], precision=PRECISE, preferred_element_type=jnp.float32)
            quad.append(jnp.sum(y * y, axis=0, keepdims=True))
        logp = jnp.log(weights) - tails[:, half : half + 1] - 0.5 * jnp.concatenate(quad, axis=0)
        resp = softmax_regimes(logp)

    memall[g] = resp
    for k in range(1, ng):
        copy = remote(memall.at[g], memall.at[g], y_send.at[k - 1], y_recv.at[g], (grid_peer(k), d))
        copy.start()
        sent.append(copy)
    mine = resp.astype(jnp.bfloat16)
    for s in range(nd):
        cacc[s] = jnp.dot(mine, anom[s, part(g), :], preferred_element_type=jnp.float32)
    o_means[...] = means
    o_weights[...] = jnp.sum(jnp.where(er == ec, weights, 0.0), axis=0)
    for k in range(1, ng):
        i = grid_peer(k)
        remote(memall.at[i], memall.at[i], y_send.at[0], y_recv.at[i], (i, d)).wait_recv()
    member = jnp.concatenate([memall[i] for i in range(ng)], axis=1)
    o_member[...] = member
    cnt[d] = jnp.broadcast_to(jnp.sum(member, axis=1, keepdims=True), (regimes, 128))
    for k in range(1, nd):
        copy = remote(cnt.at[d], cnt.at[d], n_send.at[k - 1], n_recv.at[d], (g, day_peer(k)))
        copy.start()
        sent.append(copy)

    def field_sums(s):
        def add(k, total):
            i = grid_peer(k)
            days = memall[i].astype(jnp.bfloat16)
            return total + jnp.dot(days, anom[s, part(i), :], preferred_element_type=jnp.float32)

        total = cacc[s]
        if ng > 4:
            return lax.fori_loop(1, ng, add, total)
        for k in range(1, ng):
            total = add(k, total)
        return total

    order = [lax.rem(z + o, nz) for o in reversed(offsets)] + [z]
    for n in order:
        cout[n] = field_sums(2 * n + 1 - core)
        copy = remote(cout.at[n], cin.at[n], u_send.at[n], u_recv.at[n], (g, sibling))
        copy.start()
        sent.append(copy)

    for n in range(pairs_of):
        r = 2 * n + core

        @pl.when(z != n)
        def _():
            copy = remote(cres.at[r], cres.at[r], c_fwd.at[n], c_recv.at[r], (g, sibling))
            copy.wait_recv()
            copy.start()

    for n in order:
        terms = field_sums(2 * n + core)
        remote(cin.at[n], cin.at[n], u_send.at[n], u_recv.at[n], (g, sibling)).wait_recv()
        terms = terms + cin[n]
        if n is z:
            crecv[z] = terms
        else:
            csend[n] = terms
            copy = remote(csend.at[n], crecv.at[z], t_send.at[n], t_recv.at[z], (g, 2 * n + core))
            copy.start()
            sent.append(copy)

    for n in range(pairs_of):
        r = 2 * n + 1 - core
        remote(cres.at[r], cres.at[r], c_fwd.at[n], c_recv.at[r], (g, sibling)).wait_recv()
    for r in range(regimes):
        folded = cres[r]
        o_covs[r, 0:half, :] = folded[:, 0:width]
        o_covs[r, half:width, :] = folded[:, width : 2 * width]

    for k in range(1, nd):
        s = day_peer(k)
        remote(cnt.at[s], cnt.at[s], n_send.at[0], n_recv.at[s], (g, s)).wait_recv()
    number = cnt[0]
    for s in range(1, nd):
        number = number + cnt[s]
    for n in order[:-1]:
        remote(crecv.at[n], crecv.at[n], t_send.at[n], t_recv.at[n], (g, sibling)).wait_recv()
    total = crecv[0]
    for n in range(1, nz):
        total = total + crecv[n]
    o_comp[...] = (total / jnp.maximum(number[:, 0:1], 1.0)).astype(jnp.bfloat16)

    for copy in sent:
        copy.wait_send()
    for it in range(ITERS):
        for n in range(pairs_of):
            r = 2 * n + core
            remote(msend.at[it, r], msib.at[it, n], s_send.at[it, n], s_recv.at[it, n], (g, sibling)).wait_send()

            @pl.when(z != n)
            def _():
                remote(chip.at[it, n], mrecv.at[it, z], m_send.at[it, n], m_recv.at[it, z], (g, r)).wait_send()
                remote(res.at[it, r], res.at[it, r], r_fwd.at[it, n], r_recv.at[it, r], (g, sibling)).wait_send()
                if it == ITERS - 1:
                    remote(cres.at[r], cres.at[r], c_fwd.at[n], c_recv.at[r], (g, sibling)).wait_send()

        def own_sent():
            for k in range(1, ng):
                remote(gslot.at[it, g], gslot.at[it, g], g_send.at[it, k - 1], g_recv.at[it, 0], (grid_peer(k), d)).wait_send()
            for n, target in enumerate(near):
                remote(res.at[it, d], res.at[it, d], r_send.at[it, n], r_recv.at[it, d], (g, target)).wait_send()
                if it == ITERS - 1:
                    remote(cres.at[d], cres.at[d], c_send.at[n], c_recv.at[d], (g, target)).wait_send()

        if nd > regimes:
            pl.when(d < regimes)(own_sent)
        else:
            own_sent()


def hand_over(*refs):
    n = len(refs) // 2
    for i in range(n):
        refs[n + i][...] = refs[i][...]


def solution(mesh):
    ng, nd = mesh.shape["grid"], mesh.shape["day"]

    def body(anomalies, eofs, means_init, variances, mixing):
        days, pixels = anomalies.shape
        width, pb = eofs.shape
        regimes = means_init.shape[0]
        dl = days // ng
        half = width // 2
        nz = nd // 2
        f32 = jnp.float32
        vmem = pl.BlockSpec(memory_space=pltpu.VMEM)
        dma = pltpu.SemaphoreType.DMA
        outs = pl.pallas_call(
            functools.partial(kernel, ng, nd, regimes, width, dl, pb),
            out_shape=(
                jax.ShapeDtypeStruct((regimes, width), f32),
                jax.ShapeDtypeStruct((regimes, width, width), f32),
                jax.ShapeDtypeStruct((regimes,), f32),
                jax.ShapeDtypeStruct((regimes, days), f32),
                jax.ShapeDtypeStruct((regimes, pb), jnp.bfloat16),
            ),
            in_specs=[pl.BlockSpec(memory_space=pltpu.HBM)] * 5,
            out_specs=(vmem,) * 5,
            scratch_shapes=[
                pltpu.VMEM((regimes, width), f32),
                pltpu.VMEM((regimes, width), f32),
                pltpu.VMEM((regimes,), f32),
                pltpu.VMEM((nd, days, pb), jnp.bfloat16),
                pltpu.VMEM((nd, width, pb), jnp.bfloat16),
                pltpu.VMEM((days, width), f32),
                pltpu.VMEM((ng, width, dl), f32),
                pltpu.VMEM((ng, width, dl), f32),
                pltpu.VMEM((ITERS, regimes, half + 8, 2 * width), f32),
                pltpu.VMEM((ITERS, regimes // 2, half + 8, 2 * width), f32),
                pltpu.VMEM((ITERS, regimes // 2, half + 8, 2 * width), f32),
                pltpu.VMEM((ITERS, nz, half + 8, 2 * width), f32),
                pltpu.VMEM((ITERS, ng, half + 8, 2 * width), f32),
                pltpu.VMEM((ITERS, regimes, half + 8, 2 * width), f32),
                pltpu.VMEM((regimes, half, 2 * width), f32),
                pltpu.VMEM((ng, regimes, dl), f32),
                pltpu.VMEM((nd, regimes, pb), f32),
                pltpu.VMEM((nz, regimes, pb), f32),
                pltpu.VMEM((nz, regimes, pb), f32),
                pltpu.VMEM((nz, regimes, pb), f32),
                pltpu.VMEM((nz, regimes, pb), f32),
                pltpu.VMEM((nd, regimes, 128), f32),
                dma((nd,)),
                dma((nz,)),
                dma((nz,)),
                dma((nd,)),
                dma((ng,)),
                dma((ng,)),
                dma((ITERS, regimes // 2)),
                dma((ITERS, regimes // 2)),
                dma((ITERS, regimes // 2)),
                dma((ITERS, nz)),
                dma((ITERS, ng)),
                dma((ITERS, ng)),
                dma((ITERS, nz)),
                dma((ITERS, regimes // 2)),
                dma((ITERS, regimes)),
                dma((nz,)),
                dma((regimes // 2,)),
                dma((regimes,)),
                dma((ng,)),
                dma((ng,)),
                dma((nz,)),
                dma((nz,)),
                dma((nz,)),
                dma((nz,)),
                dma((nd,)),
                dma((nd,)),
                dma((4,)),
            ],
            compiler_params=pltpu.CompilerParams(
                collective_id=0, has_side_effects=True, vmem_limit_bytes=60 * 1024 * 1024
            ),
            name="regimes",
        )(anomalies, eofs, means_init, variances, mixing)
        return pl.pallas_call(
            hand_over,
            out_shape=tuple(jax.ShapeDtypeStruct(o.shape, o.dtype) for o in outs),
            in_specs=[vmem] * len(outs),
            out_specs=(vmem,) * len(outs),
            compiler_params=pltpu.CompilerParams(vmem_limit_bytes=60 * 1024 * 1024),
            name="hand_over",
        )(*outs)

    in_specs = (P("day", "grid"), P(None, ("grid", "day")), P(), P(), P())
    out_specs = (P(), P(), P(), P(None, "day"), P(None, ("grid", "day")))
    return jax.shard_map(body, mesh=mesh, in_specs=in_specs, out_specs=out_specs, check_vma=False)
```
